256 devices in a mesh: tok: 32 (over z_hi, y, core), voc: 8 (over x, z_lo).
Axes of the slice: x: 4, y: 4, z: 8 (z_hi: 4, z_lo: 2; z = z_hi * 2 + z_lo), core: 2. Of those that a mesh axis runs over, the one named last changes fastest.
Arguments:
- hidden: bfloat16 [12288, 2304], P('tok'), may hold values from -6 to 6
- head: bfloat16 [2304, 16000], P(None, 'voc'), may hold values from -0.375 to 0.375
- teacher_logp: bfloat16 [12288, 16000], P('tok', 'voc'), may hold values from -30 to 0
- slot_blocks: int32 [128], replicated, may hold values from 0 to 127, as said below
- segment_ids: int32 [12288], P('tok'), may hold values from 0 to 63, never falling along the last dimension, each value on 1 to 768 neighbouring positions
Outputs:
- d_hidden: bfloat16 [12288, 2304], P('tok', 'voc')
- d_head: float32 [2304, 16000], P('tok', 'voc')
The draws below stay inside these ranges and needn't reach their ends.
Inputs may be any that keep to these rules, and one draw needn't show every extreme that they name: `slot_blocks`: each of the 128 blocks is named exactly once; the 16 entries of teacher voc index j (entries j * 16 to (j + 1) * 16 - 1) name exactly 2 blocks of the range k * 16 to (k + 1) * 16 - 1 for every voc index k. `segment_ids`: never falling along the tokens; each of the 64 segments has 1 to 768 tokens, one exactly 768.
All inputs are finite; a program needn't handle non-finite values.
Results may differ from the reference program's by a relative error of at most 0.025.
Values may be sent and summed in bfloat16 or wider, within the bound.
A program may use at most 128 MiB of HBM per device.

```python
import math
import jax
import jax.numpy as jnp
import numpy as np
from jax import lax

D = 2304
VOC_DEV = 2000
TOK_DEV = 384
REP = 2
SEG_DEV = 2
VOCAB = 16000
TOKENS = 12288
NB = 128
NSEG = 64
N_TOK = 32
N_VOC = 8


def draw_teacher_logp(key, part):
    key = jax.random.fold_in(key, 11)
    normal_part = jax.random.normal(key, (TOKENS, VOCAB), jnp.float32)
    values = 3.0 * jnp.clip(normal_part, -4.0, 4.0) - math.log(VOCAB) - 4.5
    return jnp.clip(values, -30.0, -0.25).astype(jnp.bfloat16)


def draw_slot_blocks(key, part):
    key = jax.random.fold_in(key, 3)
    blocks_each = N_VOC * REP
    perm_keys = jax.random.split(key, 2 * N_VOC)
    perms = jax.vmap(lambda subkey: jax.random.permutation(subkey, blocks_each))(perm_keys[:N_VOC])
    blocks = jnp.arange(N_VOC, dtype=jnp.int32)[None, :, None] * blocks_each + perms.reshape(N_VOC, N_VOC, REP).transpose(1, 0, 2).astype(jnp.int32)
    flat_blocks = blocks.reshape(N_VOC, blocks_each)
    shuffles = jax.vmap(lambda subkey: jax.random.permutation(subkey, blocks_each))(perm_keys[N_VOC:])
    mixed = jnp.take_along_axis(flat_blocks, shuffles.astype(jnp.int32), axis=1)
    return mixed.reshape(-1).astype(jnp.int32)


def block_levels(rng, shape, cuts, low, largest):
    def one(position, shards_of):
        draws = jax.random.uniform(jax.random.fold_in(jax.random.fold_in(rng, 6), position), (shards_of,), jnp.float32, low / len(cuts), largest / len(cuts))
        return jnp.repeat(jnp.exp(draws), shape[position] // shards_of).reshape((-1,) + (1,) * (len(shape) - position - 1))

    factor_of = one(*cuts[0])
    for cut in cuts[1:]:
        factor_of = factor_of * one(*cut)
    return factor_of


def length_profile(count, total, most, lean):
    weights = [(1 << 20) // math.isqrt(standing ** lean) + 1 for standing in range(2, count + 1)]
    rest, counts = total - most - (count - 1), [1] * (count - 1)
    while rest > 0:
        movable = [i for i in range(count - 1) if counts[i] < most]
        whole, budget = sum([weights[i] for i in movable]), rest
        for i in movable:
            extra = min(most - counts[i], max(1, budget * weights[i] // whole), rest)
            counts[i] = counts[i] + extra
            rest = rest - extra
    return np.array([most] + counts)


def uneven(own_key, amount, total, bound, skew):
    if amount == 2:
        one = jax.random.randint(own_key, (), max(1, total - bound), min(bound, total - 1) + 1)
        return jnp.stack([one, total - one])
    lengths = jnp.asarray(length_profile(amount, total, bound, skew), jnp.int32)
    couples = (amount - 1) // 2
    giver, receiver = lengths[1:1 + 2 * couples:2], lengths[2:2 + 2 * couples:2]
    margin = jnp.minimum(giver - 1, bound - receiver)
    passed = jax.random.randint(jax.random.fold_in(own_key, 1), (couples,), 0, 1 << 20) % (margin + 1)
    lengths = lengths.at[1:1 + 2 * couples:2].set(giver - passed).at[2:2 + 2 * couples:2].set(receiver + passed)
    return lengths[jax.random.permutation(jax.random.fold_in(own_key, 2), amount)]


def scatter_about(rng, dims, width, bound, pieces=(), held_as=jnp.bfloat16):
    values = width * jax.random.normal(rng, dims, jnp.float32)
    if pieces:
        values = values * block_levels(rng, dims, pieces, -0.22, 0.18)
    return jnp.clip(values, -bound, bound).astype(held_as)


def setup_inputs(seed: int = 0) -> dict:
    streams_of = jax.random.split(jax.random.key(seed), 6)
    hidden = scatter_about(streams_of[0], (TOKENS, D), 1.0, 6.0, ((0, 32),))
    head = scatter_about(streams_of[1], (D, VOCAB), (D // 9) ** -0.5, 0.375, ((1, 8),))
    teacher_logp = draw_teacher_logp(jax.random.fold_in(streams_of[5], 71), 0)
    slot_blocks = draw_slot_blocks(jax.random.fold_in(streams_of[5], 71), 0)
    segment_ids = jnp.searchsorted(jnp.cumsum(uneven(streams_of[4], NSEG, TOKENS, 2 * TOK_DEV, 0)), jnp.arange(TOKENS), side="right").astype(jnp.int32)
    return dict(hidden=hidden, head=head, teacher_logp=teacher_logp, slot_blocks=slot_blocks, segment_ids=segment_ids)


soft_cap = 30.0
loss_scale = 1024.0


def relay_teacher(teacher_logp, slot_blocks):
    block_cols = VOC_DEV // (N_VOC * REP)
    tile_blocks = teacher_logp.reshape(TOKENS, NB, block_cols)
    inverse = jnp.argsort(slot_blocks).astype(jnp.int32)
    return jnp.take(tile_blocks, inverse, axis=1).reshape(TOKENS, VOCAB)


def round_term(value):
    rounded = lax.optimization_barrier(value.astype(jnp.bfloat16))
    return rounded.astype(jnp.float32)


def reference(hidden, head, teacher_logp, slot_blocks, segment_ids):
    student_teacher = relay_teacher(teacher_logp, slot_blocks)
    num_segments = SEG_DEV * N_TOK
    onehot = (segment_ids[:, None] == jnp.arange(num_segments, dtype=jnp.int32)[None, :]).astype(jnp.float32)
    segment_count = jnp.sum(onehot, axis=0)
    seg_size = jnp.sum(onehot * segment_count[None, :], axis=1)
    token_weight = (TOK_DEV / SEG_DEV) / seg_size

    def one_block(head_total, inputs):
        row_block, teacher_rows, row_weight = inputs
        logits = jnp.dot(row_block, head, preferred_element_type=jnp.float32)
        capped = soft_cap * jnp.tanh(logits / soft_cap)
        shifted = jnp.exp(capped - soft_cap)
        student_total = jnp.sum(shifted, axis=1, keepdims=True)
        teacher_prob = jnp.exp(teacher_rows.astype(jnp.float32))
        teacher_mass = jnp.sum(teacher_prob, axis=1, keepdims=True)
        grad_logits = (loss_scale * row_weight[:, None] * (shifted / student_total * teacher_mass - teacher_prob)
                       * (1.0 - (capped / soft_cap) ** 2)).astype(jnp.bfloat16)
        hidden_sum = jnp.zeros((TOK_DEV, D), jnp.float32)
        for shard in range(N_VOC):
            grad_cols = grad_logits[:, shard * VOC_DEV:(shard + 1) * VOC_DEV]
            head_cols = head[:, shard * VOC_DEV:(shard + 1) * VOC_DEV]
            hidden_sum = hidden_sum + round_term(jnp.dot(grad_cols, head_cols.T, preferred_element_type=jnp.float32))
        hidden_grad = hidden_sum.astype(jnp.bfloat16)
        head_total = head_total + round_term(jnp.dot(row_block.T, grad_logits, preferred_element_type=jnp.float32))
        return head_total, hidden_grad

    scan_inputs = (hidden.reshape(N_TOK, TOK_DEV, D),
                   student_teacher.reshape(N_TOK, TOK_DEV, VOCAB),
                   token_weight.reshape(N_TOK, TOK_DEV))
    d_head, hidden_grad = lax.scan(one_block, jnp.zeros((D, VOCAB), jnp.float32), scan_inputs)
    return hidden_grad.reshape(TOKENS, D), d_head
```

```python
import jax
import jax.numpy as jnp
from jax import lax
from jax.experimental import pallas as pl
from jax.experimental.pallas import tpu as pltpu
from jax.sharding import PartitionSpec as P

MESH = pl.DeviceIdType.MESH
F32 = jnp.float32
BF16 = jnp.bfloat16

NTOK = 32
NVOC = 8
T = 384
D = 2304
V = 2000
NBLK = 16
BC = 125
LAST = V - 15 * 128
R = D // NTOK
RY = 4 * R
RV = D // NVOC
SEGS = 64
SEG_WEIGHT = 192.0
CAP = 30.0
SCALE = 1024.0

LAG_C1 = 2
LAG_C2 = 3
LAG_C3 = 4
LAG_C4 = 5
TICKS = 8 + LAG_C4
TICK_H = 4


def dot(a, b):
    return jnp.dot(a, b, preferred_element_type=F32)


def dot_nt(a, b):
    return lax.dot_general(a, b, (((1,), (1,)), ((), ())), preferred_element_type=F32)


def kernel(
    slot, seg, hid_h, head_h, tea_h, dhid_o, dhead_o,
    tea_v, hid_v, head_v, headl, tblk, tsend, trec, idb, h32, hsend, ht, lnat,
    pblk, qblk, acc_t, acc_m, tots, arow, wrow, gc, gslot, gnat,
    yfar_s, yfar_r, ydir_s, ydir_r, yst_s, yst_r, ymid, yown,
    zfar_s, zfar_r, zdir_s, zdir_r, zst_s, zst_r, fin,
    xfar_s, xfar_r, xdir_s, xdir_r, xst_s, xst_r, xmid, xown, zl_s, zl_r,
    snd, blk, inv,
    lsem, id_ss, id_rs, t_ss, t_rs, ht_ss, ht_rs, tot_ss, tot_rs, g_ss, g_rs,
    yfar_ss, yfar_rs, ydir_ss, ydir_rs, yst_ss, yst_rs,
    zfar_ss, zfar_rs, zdir_ss, zdir_rs, zst_ss, zst_rs,
    xfar_ss, xfar_rs, xdir_ss, xdir_rs, xst_ss, xst_rs, zl_ss, zl_rs,
):
    t = lax.axis_index("tok")
    v = lax.axis_index("voc")
    c = lax.rem(t, 2)
    y = lax.rem(lax.div(t, 2), 4)
    zh = lax.div(t, 8)
    x = lax.div(v, 2)
    zl = lax.rem(v, 2)

    def at_y(step):
        return (zh * 8 + lax.rem(y + step + 4, 4) * 2 + c, v)

    def at_z(step):
        return (lax.rem(zh + step + 4, 4) * 8 + y * 2 + c, v)

    def at_x(step):
        return (t, lax.rem(x + step + 4, 4) * 2 + zl)

    sibling = (t + 1 - 2 * c, v)
    zl_peer = (t, v + 1 - 2 * zl)

    def at_v(step):
        return (t, lax.rem(v + step, NVOC))

    def at_t(step):
        return (lax.rem(t + step + NTOK, NTOK), v)

    def send(src, dst, ss, rs, device):
        return pltpu.make_async_remote_copy(
            src_ref=src, dst_ref=dst, send_sem=ss, recv_sem=rs, device_id=device, device_id_type=MESH
        )

    id_steps = (1, -1, 2, -2)

    barrier = pltpu.get_barrier_semaphore()
    partners = [sibling, at_y(1), at_y(-1), at_z(1), at_z(-1)]
    partners += [at_v(s) for s in range(1, NVOC)] + [at_t(s) for s in id_steps]
    for device in partners:
        pl.semaphore_signal(barrier, inc=1, device_id=device, device_id_type=MESH)

    tea_copy = pltpu.make_async_copy(tea_h, tea_v, lsem.at[0])
    hid_copy = pltpu.make_async_copy(hid_h, hid_v, lsem.at[1])
    head_copy = pltpu.make_async_copy(head_h, head_v, lsem.at[2])
    tea_copy.start()
    hid_copy.start()
    head_copy.start()

    @pl.loop(0, NVOC)
    def _(d):
        low = lax.rem(v + d, NVOC) * NBLK
        first = jnp.int32(0)
        last = jnp.int32(0)
        for j in range(NBLK):
            e = slot[v * NBLK + j]
            last = jnp.where((e >= low) & (e < low + NBLK), j, last)
            e = slot[v * NBLK + NBLK - 1 - j]
            first = jnp.where((e >= low) & (e < low + NBLK), NBLK - 1 - j, first)
        snd[2 * d] = first
        snd[2 * d + 1] = last

    @pl.loop(0, NVOC)
    def _(k):
        base = lax.rem(v + k, NVOC) * NBLK
        low = v * NBLK
        first = jnp.int32(0)
        last = jnp.int32(0)
        for j in range(NBLK):
            e = slot[base + j]
            last = jnp.where((e >= low) & (e < low + NBLK), e - low, last)
            e = slot[base + NBLK - 1 - j]
            first = jnp.where((e >= low) & (e < low + NBLK), e - low, first)
        blk[2 * k] = first
        blk[2 * k + 1] = last

    @pl.loop(0, NBLK)
    def _(b):
        place = jnp.int32(0)
        for s in range(NBLK):
            place = jnp.where(blk[s] == b, s, place)
        inv[b] = place

    idb[0] = jnp.broadcast_to(seg[...], (8, T))

    tea_copy.wait()

    @pl.loop(0, T // 64)
    def _(i):
        rows = pl.ds(pl.multiple_of(i * 64, 64), 64)
        lane = lax.broadcasted_iota(jnp.int32, (64, 128), 1)
        mass = jnp.zeros((64, 128), F32)
        before = None
        for b in range(NBLK):
            if b < 15:
                tile = tea_v[rows, b * 128 : b * 128 + 128].astype(F32)
                mass += jnp.exp(tile)
            else:
                tile = jnp.concatenate(
                    [tea_v[rows, 1920:V].astype(F32), jnp.zeros((64, 128 - LAST), F32)], axis=1
                )
                mass += jnp.where(lane < LAST, jnp.exp(tile), 0.0)
            block = tile
            if b > 0:
                block = pltpu.roll(jnp.where(lane >= 128 - 3 * b, before, tile), 3 * b, 1)
            tblk[b, rows, :] = block.astype(BF16)
            before = tile
        acc_m[rows, :] = mass

    for d in range(NVOC):
        for r in range(2):
            target = trec.at[0] if d == 0 else tsend.at[d]
            target[:, r * 128 : r * 128 + 128] = tblk[snd[2 * d + r]]

    def tea_send(d):
        return send(tsend.at[d], trec.at[NVOC - d], t_ss.at[d], t_rs.at[NVOC - d], at_v(d))

    def id_send(i):
        return send(idb.at[0], idb.at[i + 1], id_ss.at[i], id_rs.at[i], at_t(id_steps[i]))

    pl.semaphore_wait(barrier, len(partners))
    for i in range(4):
        id_send(i).start()
    for d in range(NVOC - 1, 4, -1):
        tea_send(d).start()

    hid_copy.wait()

    @pl.loop(0, D // 128)
    def _(j):
        off = pl.multiple_of(j * 128, 128)
        h32[pl.ds(off, 128), :] = hid_v[:, pl.ds(off, 128)].astype(F32).T

    def pack(core, yy):
        parts = []
        for z in range(4):
            parts.append(h32[pl.ds(pl.multiple_of((8 * z + 2 * yy + core) * R, 8), R), :])
        return jnp.concatenate(parts, axis=0).astype(BF16)

    @pl.loop(0, 4)
    def _(yy):
        hsend[yy] = pack(1 - c, yy)

    ht_send = send(hsend, ht.at[:, :, pl.ds(T, T)], ht_ss, ht_rs, sibling)
    ht_send.start()

    @pl.loop(0, 4)
    def _(yy):
        ht[yy, :, 0:T] = pack(c, yy)

    head_copy.wait()
    headl[...] = jnp.concatenate([head_v[:, 1920:V], jnp.zeros((D, 128 - LAST), BF16)], axis=1)

    @pl.loop(0, 7)
    def _(j):
        cols = pl.ds(pl.multiple_of(j * 256, 256), 256)
        lnat[:, cols] = dot(hid_v[...], head_v[:, cols])

    lnat[:, 1792:2048] = dot(
        hid_v[...], jnp.concatenate([head_v[:, 1792:1920], headl[...]], axis=1)
    )

    @pl.loop(0, T // 64)
    def _(i):
        rows = pl.ds(pl.multiple_of(i * 64, 64), 64)
        lane = lax.broadcasted_iota(jnp.int32, (64, 128), 1)
        total = jnp.zeros((64, 128), F32)
        for b in range(NBLK):
            logit = lnat[rows, b * 128 : b * 128 + 128]
            if b > 0:
                before = lnat[rows, b * 128 - 128 : b * 128]
                logit = pltpu.roll(jnp.where(lane >= 128 - 3 * b, before, logit), 3 * b, 1)
            th = jnp.tanh(logit * (1.0 / CAP))
            shifted = jnp.exp(CAP * th - CAP)
            slope = 1.0 - th * th
            total += jnp.where(lane < BC, shifted, 0.0)
            pblk[b, rows, :] = shifted * slope
            qblk[b, rows, :] = slope
        acc_t[rows, :] = total

    sub = lax.broadcasted_iota(jnp.int32, (8, T), 0)
    total_row = jnp.sum(acc_t[...].T, axis=0, keepdims=True)
    mass_row = jnp.sum(acc_m[...].T, axis=0, keepdims=True)
    tots[0] = jnp.where(sub == 0, total_row, mass_row)

    def tot_send(d):
        return send(tots.at[0], tots.at[NVOC - d], tot_ss.at[d], tot_rs.at[NVOC - d], at_v(d))

    for d in range(1, NVOC):
        tot_send(d).start()
    for d in range(4, 0, -1):
        tea_send(d).start()

    for i in range(4):
        id_send(i).wait_recv()
    segments = lax.broadcasted_iota(jnp.int32, (SEGS, T), 0)
    own_hit = segments == idb[0, 0:1, :]
    hits = own_hit.astype(F32)
    for i in range(1, 5):
        hits += (segments == idb[i, 0:1, :]).astype(F32)
    counts = jnp.sum(hits, axis=1, keepdims=True)
    seg_size = jnp.sum(jnp.where(own_hit, counts, 0.0), axis=0, keepdims=True)
    weight = (SCALE * SEG_WEIGHT) / seg_size
    wrow[...] = jnp.broadcast_to(weight, (128, T)).T

    for d in range(1, NVOC):
        tot_send(NVOC - d).wait_recv()
    sums = tots[0]
    for d in range(1, NVOC):
        sums += tots[d]
    ratio = weight * (sums[1:2, :] / sums[0:1, :])
    arow[...] = jnp.broadcast_to(ratio, (128, T)).T

    ht_send.wait_recv()

    def g_send(k):
        return send(
            gc.at[k, pl.ds(0, T), :], gc.at[k, pl.ds(T, T), :], g_ss.at[k], g_rs.at[k], sibling
        )

    def yfar(k, r):
        return send(yfar_s.at[k, r], yfar_r.at[k, r], yfar_ss.at[k, r], yfar_rs.at[k, r], at_y(1 - 2 * r))

    def ydir(k, r):
        return send(ydir_s.at[k, r], ydir_r.at[k, r], ydir_ss.at[k, r], ydir_rs.at[k, r], at_y(2 * r - 1))

    def yst(k, r):
        return send(yst_s.at[k, r], yst_r.at[k, r], yst_ss.at[k, r], yst_rs.at[k, r], at_y(1 - 2 * r))

    def zway(k):
        return 1 - 2 * lax.rem(k, 2)

    def zfar(k):
        return send(zfar_s.at[k], zfar_r.at[k], zfar_ss.at[k], zfar_rs.at[k], at_z(zway(k)))

    def zdir(k):
        return send(zdir_s.at[k], zdir_r.at[k], zdir_ss.at[k], zdir_rs.at[k], at_z(-zway(k)))

    def zst(k):
        return send(zst_s.at[k], zst_r.at[k], zst_ss.at[k], zst_rs.at[k], at_z(zway(k)))

    def grads(k):
        @pl.when(k > 0)
        def _():
            tea_send(NVOC - k).wait_recv()

        @pl.loop(0, T // 128)
        def _(i):
            rows = pl.ds(pl.multiple_of(i * 128, 128), 128)
            for r in range(2):
                b = blk[2 * k + r]
                prob = jnp.exp(trec[k, rows, r * 128 : r * 128 + 128].astype(F32))
                grad = arow[rows, :] * pblk[b, rows, :] - wrow[rows, :] * prob * qblk[b, rows, :]
                grad = grad.astype(BF16)
                gc[k, rows, r * 128 : r * 128 + 128] = grad
                gslot[2 * k + r, rows, :] = grad

        g_send(k).start()

    def mm(k):
        g_send(k).wait_recv()
        far = dot(ht[lax.rem(y + 2, 4)], gc[k])
        for r in range(2):
            yfar_s[k, r] = far[:, r * 128 : r * 128 + 128].astype(BF16)
            yfar(k, r).start()
        part = dot(ht[lax.rem(y + 1, 4)], gc[k])
        ydir_s[k, 1] = part[:, 128:].astype(BF16)
        ydir(k, 1).start()
        ymid[k, 0] = part[:, :128]
        part = dot(ht[lax.rem(y + 3, 4)], gc[k])
        ydir_s[k, 0] = part[:, :128].astype(BF16)
        ydir(k, 0).start()
        ymid[k, 1] = part[:, 128:]
        yown[k] = dot(ht[y], gc[k])

    def c1(k):
        for r in range(2):
            yfar(k, r).wait_recv()
            yst_s[k, r] = (ymid[k, r] + yfar_r[k, r].astype(F32)).astype(BF16)
            yst(k, r).start()

    def zrows(k, step):
        rows = pl.ds(pl.multiple_of(lax.rem(zh + step + 4, 4) * R, 8), R)
        return jnp.concatenate([yown[k, rows, 0:128], yown[k, rows, 128:256]], axis=0)

    def c2(k):
        for r in range(2):
            ydir(k, r).wait_recv()
            yst(k, r).wait_recv()
            lanes = slice(r * 128, r * 128 + 128)
            yown[k, :, lanes] += ydir_r[k, r].astype(F32) + yst_r[k, r].astype(F32)
        zfar_s[k] = zrows(k, 2).astype(BF16)
        zfar(k).start()
        zdir_s[k] = zrows(k, -zway(k)).astype(BF16)
        zdir(k).start()

    def c3(k):
        zfar(k).wait_recv()
        zst_s[k] = (zrows(k, zway(k)) + zfar_r[k].astype(F32)).astype(BF16)
        zst(k).start()

    def c4(k):
        zdir(k).wait_recv()
        zst(k).wait_recv()
        done = zrows(k, 0) + (zdir_r[k].astype(F32) + zst_r[k].astype(F32))
        fin[2 * k] = done[0:R]
        fin[2 * k + 1] = done[R : 2 * R]

    def xfar(h):
        return send(xfar_s.at[h], xfar_r.at[h], xfar_ss.at[h], xfar_rs.at[h], at_x(1 - 2 * h))

    def xdir(h):
        return send(xdir_s.at[h], xdir_r.at[h], xdir_ss.at[h], xdir_rs.at[h], at_x(2 * h - 1))

    def xst(h):
        return send(xst_s.at[h], xst_r.at[h], xst_ss.at[h], xst_rs.at[h], at_x(1 - 2 * h))

    zlx = send(zl_s, zl_r, zl_ss, zl_rs, zl_peer)

    def natural():
        @pl.loop(0, T // 64)
        def _(i):
            rows = pl.ds(pl.multiple_of(i * 64, 64), 64)
            lane = lax.broadcasted_iota(jnp.int32, (64, 128), 1)

            def rolled(b):
                s = inv[b]
                block = gslot[s, rows, :].astype(F32)
                return pltpu.roll(block, 128 - 3 * b, 1) if b else block

            here = rolled(0)
            for q in range(NBLK):
                after = rolled(q + 1) if q < 15 else jnp.zeros((64, 128), F32)
                gnat[rows, q * 128 : q * 128 + 128] = jnp.where(
                    lane < BC - 3 * q, here, after
                ).astype(BF16)
                here = after

    def part_h(step, h):
        rows = pl.ds(pl.multiple_of((lax.rem(x + step, 4) * 2 + h) * RV, 16), RV)
        return dot_nt(head_v[rows, 0:1920], gnat[:, 0:1920]) + dot_nt(headl[rows, :], gnat[:, 1920:2048])

    def h0():
        natural()
        for h in range(2):
            xfar_s[h] = part_h(2, h).astype(BF16)
            xfar(h).start()
        xdir_s[1] = part_h(1, 1).astype(BF16)
        xdir(1).start()
        xdir_s[0] = part_h(3, 0).astype(BF16)
        xdir(0).start()

    def h1():
        xmid[0] = part_h(1, 0)
        xmid[1] = part_h(3, 1)
        for h in range(2):
            xfar(h).wait_recv()
            xst_s[h] = (xmid[h] + xfar_r[h].astype(F32)).astype(BF16)
            xst(h).start()
        for h in range(2):
            xown[h] = part_h(0, h)

    def h2():
        for h in range(2):
            xdir(h).wait_recv()
            xst(h).wait_recv()
            xown[h] += xdir_r[h].astype(F32) + xst_r[h].astype(F32)
        zl_s[...] = xown[1 - zl].astype(BF16)
        zlx.start()

    def h3():
        zlx.wait_recv()
        full = xown[zl] + zl_r[...].astype(F32)
        dhid_o[...] = full.T.astype(BF16)

    @pl.loop(0, TICKS)
    def _(n):
        def stage(f, lag):
            @pl.when((n >= lag) & (n < lag + NVOC))
            def _():
                f(n - lag)

        stage(c1, LAG_C1)

        @pl.when(n < 4)
        def _():
            grads(2 * n)
            grads(2 * n + 1)

        stage(mm, 0)
        stage(c2, LAG_C2)
        stage(c3, LAG_C3)
        stage(c4, LAG_C4)
        pl.when(n == TICK_H)(h0)
        pl.when(n == TICK_H + 1)(h1)
        pl.when(n == TICK_H + 4)(h2)
        pl.when(n == TICK_H + 6)(h3)

    lane = lax.broadcasted_iota(jnp.int32, (R, 128), 1)

    def rolled_out(b):
        block = fin[inv[b]]
        return pltpu.roll(block, 128 - 3 * b, 1) if b else block

    here = rolled_out(0)
    for q in range(NBLK):
        after = rolled_out(q + 1) if q < 15 else here
        tile = jnp.where(lane < BC - 3 * q, here, after)
        if q < 15:
            dhead_o[:, q * 128 : q * 128 + 128] = tile
        else:
            dhead_o[:, 1920:V] = tile[:, 0:LAST]
        here = after

    for i in range(4):
        id_send(i).wait_send()
    for d in range(1, NVOC):
        tea_send(d).wait_send()
        tot_send(d).wait_send()
    ht_send.wait_send()

    @pl.loop(0, NVOC)
    def _(k):
        g_send(k).wait_send()
        for r in range(2):
            yfar(k, r).wait_send()
            ydir(k, r).wait_send()
            yst(k, r).wait_send()
        zfar(k).wait_send()
        zdir(k).wait_send()
        zst(k).wait_send()

    for h in range(2):
        xfar(h).wait_send()
        xdir(h).wait_send()
        xst(h).wait_send()
    zlx.wait_send()


def body(hidden, head, teacher_logp, slot_blocks, segment_ids):
    vm = pltpu.VMEM
    dma = pltpu.SemaphoreType.DMA
    chunk = (NVOC, 2)
    scratch = [
        vm((T, V), BF16),
        vm((T, D), BF16),
        vm((D, V), BF16),
        vm((D, 128), BF16),
        vm((NBLK, T, 128), BF16),
        vm((NVOC, T, 256), BF16),
        vm((NVOC, T, 256), BF16),
        vm((5, 8, T), jnp.int32),
        vm((D, T), F32),
        vm((4, RY, T), BF16),
        vm((4, RY, 2 * T), BF16),
        vm((T, 2048), F32),
        vm((NBLK, T, 128), F32),
        vm((NBLK, T, 128), F32),
        vm((T, 128), F32),
        vm((T, 128), F32),
        vm((NVOC, 8, T), F32),
        vm((T, 128), F32),
        vm((T, 128), F32),
        vm((NVOC, 2 * T, 256), BF16),
        vm((NBLK, T, 128), BF16),
        vm((T, 2048), BF16),
    ]
    scratch += [vm(chunk + (RY, 128), BF16)] * 6
    scratch += [vm(chunk + (RY, 128), F32), vm((NVOC, RY, 256), F32)]
    scratch += [vm((NVOC, 2 * R, 128), BF16)] * 6
    scratch += [vm((NBLK, R, 128), F32)]
    scratch += [vm((2, RV, T), BF16)] * 6
    scratch += [vm((2, RV, T), F32)] * 2
    scratch += [vm((RV, T), BF16)] * 2
    scratch += [pltpu.SMEM((NBLK,), jnp.int32)] * 3
    scratch += [dma((3,)), dma((4,)), dma((4,)), dma((NVOC,)), dma((NVOC,)), dma(()), dma(())]
    scratch += [dma((NVOC,))] * 4
    scratch += [dma(chunk)] * 6 + [dma((NVOC,))] * 6 + [dma((2,))] * 6 + [dma(())] * 2
    anywhere = pl.BlockSpec(memory_space=pl.ANY)
    in_vmem = pl.BlockSpec(memory_space=pltpu.VMEM)
    return pl.pallas_call(
        kernel,
        out_shape=(
            jax.ShapeDtypeStruct((T, RV), BF16),
            jax.ShapeDtypeStruct((R, V), F32),
        ),
        in_specs=[pl.BlockSpec(memory_space=pltpu.SMEM), in_vmem, anywhere, anywhere, anywhere],
        out_specs=(in_vmem, in_vmem),
        scratch_shapes=scratch,
        compiler_params=pltpu.CompilerParams(
            collective_id=0, has_side_effects=True, vmem_limit_bytes=63 * 2**20
        ),
    )(slot_blocks, segment_ids.reshape(1, T), hidden, head, teacher_logp)


def solution(mesh):
    placed = (P("tok", None), P(None, "voc"), P("tok", "voc"), P(), P("tok"))
    return jax.shard_map(
        body,
        mesh=mesh,
        in_specs=placed,
        out_specs=(P("tok", "voc"), P("tok", "voc")),
        check_vma=False,
    )
```

```python
import jax
import jax.numpy as jnp
from jax import lax
from jax.experimental import pallas as pl
from jax.experimental.pallas import tpu as pltpu
from jax.sharding import PartitionSpec as P

MESH = pl.DeviceIdType.MESH
F32 = jnp.float32
BF16 = jnp.bfloat16

NTOK = 32
NVOC = 8
T = 384
D = 2304
V = 2000
VP = 2048
NBLK = 16
BC = 125
LAST = V - 15 * 128
R = D // NTOK
RY = 4 * R
RV = D // NVOC
SEGS = 64
SEG_WEIGHT = 192.0
CAP = 30.0
SCALE = 1024.0

ORDER = (0, 1, 2, 7, 6, 3, 4, 5)
AHEAD = 8
LAG_C1 = 2
LAG_C2 = 3
LAG_C3 = 4
LAG_C4 = 5
TICKS = 8 + LAG_C4
TICK_H = 4


def dot(a, b):
    return jnp.dot(a, b, preferred_element_type=F32)


def dot_nt(a, b):
    return lax.dot_general(a, b, (((1,), (1,)), ((), ())), preferred_element_type=F32)


def kernel(
    slot, seg, hid_h, head_h, tea_h, dhid_o, dhead_o,
    tea_v, hid_v, head_v, tea32, nat32, tblk, tsend, trec, idb, h32, htn, hsend, ht,
    pblk, qblk, tots, arow, wrow, gc, gslot, gnat,
    yfar_s, yfar_r, ydir_s, ydir_r, yst_s, yst_r, ymid, yown,
    zfar_s, zfar_r, zdir_s, zdir_r, zst_s, zst_r, fin,
    xfar_s, xfar_r, xdir_s, xdir_r, xst_s, xst_r, xmid, xown, zl_s, zl_r,
    snd, blk, inv,
    lsem, hd_sem, id_ss, id_rs, t_ss, t_rs, ht_ss, ht_rs, tot_ss, tot_rs, g_ss, g_rs,
    yfar_ss, yfar_rs, ydir_ss, ydir_rs, yst_ss, yst_rs,
    zfar_ss, zfar_rs, zdir_ss, zdir_rs, zst_ss, zst_rs,
    xfar_ss, xfar_rs, xdir_ss, xdir_rs, xst_ss, xst_rs, zl_ss, zl_rs,
):
    t = lax.axis_index("tok")
    v = lax.axis_index("voc")
    c = lax.rem(t, 2)
    y = lax.rem(lax.div(t, 2), 4)
    zh = lax.div(t, 8)
    x = lax.div(v, 2)
    zl = lax.rem(v, 2)

    def at_y(step):
        return (zh * 8 + lax.rem(y + step + 4, 4) * 2 + c, v)

    def at_z(step):
        return (lax.rem(zh + step + 4, 4) * 8 + y * 2 + c, v)

    def at_x(step):
        return (t, lax.rem(x + step + 4, 4) * 2 + zl)

    sibling = (t + 1 - 2 * c, v)
    zl_peer = (t, v + 1 - 2 * zl)

    def at_v(step):
        return (t, lax.rem(v + step, NVOC))

    def at_t(step):
        return (lax.rem(t + step + NTOK, NTOK), v)

    def send(src, dst, ss, rs, device):
        return pltpu.make_async_remote_copy(
            src_ref=src, dst_ref=dst, send_sem=ss, recv_sem=rs, device_id=device, device_id_type=MESH
        )

    id_steps = (1, -1, 2, -2)

    barrier = pltpu.get_barrier_semaphore()
    partners = [sibling, at_y(1), at_y(-1), at_z(1), at_z(-1)]
    partners += [at_v(s) for s in range(1, NVOC)] + [at_t(s) for s in id_steps]
    for device in partners:
        pl.semaphore_signal(barrier, inc=1, device_id=device, device_id_type=MESH)

    tea_copy = pltpu.make_async_copy(tea_h, tea_v.at[pl.ds(0, V)], lsem.at[0])
    hid_copy = pltpu.make_async_copy(hid_h, hid_v, lsem.at[1])

    def head_copy(p):
        rows = pl.ds(p * 512, min(512, V - p * 512))
        return pltpu.make_async_copy(head_h.at[rows], head_v.at[rows], hd_sem.at[p])

    tea_copy.start()
    hid_copy.start()

    idb[0] = jnp.broadcast_to(seg[...].reshape(1, T), (8, T))

    tea_v[V:VP, :] = jnp.zeros((VP - V, T), BF16)
    head_v[V:VP, :] = jnp.zeros((VP - V, D), BF16)
    tea_copy.wait()
    head_copy(0).start()
    head_copy(1).start()

    def fold(values):
        return jnp.sum(values.reshape(values.shape[0] // 8, 8, T), axis=0)

    def tea_step(i, mass):
        rows = pl.ds(pl.multiple_of(i * 80, 80), 80)
        tile = tea_v[rows, :].astype(F32)
        tea32[rows, :] = tile
        return mass + fold(jnp.exp(tile))

    mass_part = lax.fori_loop(0, V // 80, tea_step, jnp.zeros((8, T), F32))
    tea32[V:VP, :] = jnp.zeros((VP - V, T), F32)

    hid_copy.wait()

    @pl.loop(0, D // 128)
    def _(j):
        off = pl.multiple_of(j * 128, 128)
        turned = hid_v[:, pl.ds(off, 128)].astype(F32).T
        h32[pl.ds(off, 128), :] = turned
        htn[pl.ds(off, 128), :] = turned.astype(BF16)

    total_part = jnp.zeros((8, T), F32)
    valid = lax.broadcasted_iota(jnp.int32, (128, T), 0) < BC
    for b in range(NBLK):
        if b % 4 == 0:
            head_copy(b // 4).wait()
            if b < 8:
                head_copy(b // 4 + 2).start()
        nat32[b * 128 : b * 128 + 128, :] = dot(head_v[b * 128 : b * 128 + 128, :], htn[...])
        th = jnp.tanh(nat32[b * BC : b * BC + 128, :] * (1.0 / CAP))
        shifted = jnp.exp(CAP * th - CAP)
        slope = 1.0 - th * th
        pblk[b] = shifted * slope
        qblk[b] = slope
        total_part += fold(jnp.where(valid, shifted, 0.0))

    sub = lax.broadcasted_iota(jnp.int32, (8, T), 0)
    total_row = jnp.sum(total_part, axis=0, keepdims=True)
    mass_row = jnp.sum(mass_part, axis=0, keepdims=True)
    tots[0] = jnp.where(sub == 0, total_row, mass_row)

    def tot_send(d):
        return send(tots.at[0], tots.at[NVOC - d], tot_ss.at[d], tot_rs.at[NVOC - d], at_v(d))

    pl.semaphore_wait(barrier, len(partners))
    for d in range(1, NVOC):
        tot_send(d).start()

    def tea_send(k):
        back = NVOC - (ORDER[k] if isinstance(k, int) else offset(k))
        return send(tsend.at[k], trec.at[k], t_ss.at[k], t_rs.at[k], at_v(back))

    def id_send(i):
        return send(idb.at[0], idb.at[i + 1], id_ss.at[i], id_rs.at[i], at_t(id_steps[i]))

    for i in range(4):
        id_send(i).start()

    def pack(core, yy):
        parts = []
        for z in range(4):
            parts.append(h32[pl.ds(pl.multiple_of((8 * z + 2 * yy + core) * R, 8), R), :])
        return jnp.concatenate(parts, axis=0).astype(BF16)

    @pl.loop(0, 4)
    def _(yy):
        hsend[yy] = pack(1 - c, yy)

    ht_send = send(hsend, ht.at[:, :, pl.ds(T, T)], ht_ss, ht_rs, sibling)
    ht_send.start()

    @pl.loop(0, 4)
    def _(yy):
        ht[yy, :, 0:T] = pack(c, yy)

    def offset(k):
        out = jnp.int32(0)
        for i in range(1, NVOC):
            out = jnp.where(k == i, ORDER[i], out)
        return out

    @pl.loop(0, NVOC)
    def _(d):
        low = lax.rem(v + NVOC - offset(d), NVOC) * NBLK
        first = jnp.int32(0)
        last = jnp.int32(0)
        for j in range(NBLK):
            e = slot[v * NBLK + j]
            last = jnp.where((e >= low) & (e < low + NBLK), j, last)
            e = slot[v * NBLK + NBLK - 1 - j]
            first = jnp.where((e >= low) & (e < low + NBLK), NBLK - 1 - j, first)
        snd[2 * d] = first
        snd[2 * d + 1] = last

    for b in range(NBLK):
        tblk[b] = tea32[b * BC : b * BC + 128, :].astype(BF16)

    for d in range(NVOC):
        for r in range(2):
            target = trec.at[0] if d == 0 else tsend.at[d]
            target[r * 128 : r * 128 + 128, :] = tblk[snd[2 * d + r]]

    for k in range(1, AHEAD):
        tea_send(k).start()

    @pl.loop(0, NVOC)
    def _(k):
        base = lax.rem(v + offset(k), NVOC) * NBLK
        low = v * NBLK
        first = jnp.int32(0)
        last = jnp.int32(0)
        for j in range(NBLK):
            e = slot[base + j]
            last = jnp.where((e >= low) & (e < low + NBLK), e - low, last)
            e = slot[base + NBLK - 1 - j]
            first = jnp.where((e >= low) & (e < low + NBLK), e - low, first)
        blk[2 * k] = first
        blk[2 * k + 1] = last

    @pl.loop(0, NBLK)
    def _(b):
        place = jnp.int32(0)
        for s in range(NBLK):
            place = jnp.where(blk[s] == b, s, place)
        inv[b] = place

    for i in range(4):
        id_send(i).wait_recv()
    segments = lax.broadcasted_iota(jnp.int32, (SEGS, T), 0)
    own_hit = segments == idb[0, 0:1, :]
    hits = own_hit.astype(F32)
    for i in range(1, 5):
        hits += (segments == idb[i, 0:1, :]).astype(F32)
    counts = jnp.sum(hits, axis=1, keepdims=True)
    seg_size = jnp.sum(jnp.where(own_hit, counts, 0.0), axis=0, keepdims=True)
    weight = (SCALE * SEG_WEIGHT) / seg_size
    wrow[...] = jnp.broadcast_to(weight, (8, T))

    for d in range(1, NVOC):
        tot_send(NVOC - d).wait_recv()
    sums = tots[0]
    for d in range(1, NVOC):
        sums += tots[d]
    ratio = weight * (sums[1:2, :] / sums[0:1, :])
    arow[...] = jnp.broadcast_to(ratio, (8, T))

    for k in range(AHEAD, NVOC):
        tea_send(k).start()
    ht_send.wait_recv()

    def g_send(k):
        return send(
            gc.at[k, pl.ds(0, T), :], gc.at[k, pl.ds(T, T), :], g_ss.at[k], g_rs.at[k], sibling
        )

    def yfar(k, r):
        return send(yfar_s.at[k, r], yfar_r.at[k, r], yfar_ss.at[k, r], yfar_rs.at[k, r], at_y(1 - 2 * r))

    def ydir(k, r):
        return send(ydir_s.at[k, r], ydir_r.at[k, r], ydir_ss.at[k, r], ydir_rs.at[k, r], at_y(2 * r - 1))

    def yst(k, r):
        return send(yst_s.at[k, r], yst_r.at[k, r], yst_ss.at[k, r], yst_rs.at[k, r], at_y(1 - 2 * r))

    def zway(k):
        return 1 - 2 * lax.rem(k, 2)

    def zfar(k):
        return send(zfar_s.at[k], zfar_r.at[k], zfar_ss.at[k], zfar_rs.at[k], at_z(zway(k)))

    def zdir(k):
        return send(zdir_s.at[k], zdir_r.at[k], zdir_ss.at[k], zdir_rs.at[k], at_z(-zway(k)))

    def zst(k):
        return send(zst_s.at[k], zst_r.at[k], zst_ss.at[k], zst_rs.at[k], at_z(zway(k)))

    def grads(k):
        @pl.when(k > 0)
        def _():
            tea_send(k).wait_recv()

        for r in range(2):
            b = blk[2 * k + r]
            prob = jnp.exp(trec[k, r * 128 : r * 128 + 128, :].astype(F32))
            grad = arow[0:1, :] * pblk[b] - wrow[0:1, :] * (prob * qblk[b])
            grad = grad.T.astype(BF16)
            gc[k, 0:T, r * 128 : r * 128 + 128] = grad
            gslot[2 * k + r] = grad

        g_send(k).start()

    def mm(k):
        g_send(k).wait_recv()
        far = dot(ht[lax.rem(y + 2, 4)], gc[k])
        for r in range(2):
            yfar_s[k, r] = far[:, r * 128 : r * 128 + 128].astype(BF16)
            yfar(k, r).start()
        part = dot(ht[lax.rem(y + 1, 4)], gc[k])
        ydir_s[k, 1] = part[:, 128:].astype(BF16)
        ydir(k, 1).start()
        ymid[k, 0] = part[:, :128]
        part = dot(ht[lax.rem(y + 3, 4)], gc[k])
        ydir_s[k, 0] = part[:, :128].astype(BF16)
        ydir(k, 0).start()
        ymid[k, 1] = part[:, 128:]
        yown[k] = dot(ht[y], gc[k])

    def c1(k):
        for r in range(2):
            yfar(k, r).wait_recv()
            yst_s[k, r] = (ymid[k, r] + yfar_r[k, r].astype(F32)).astype(BF16)
            yst(k, r).start()

    def zrows(k, step):
        rows = pl.ds(pl.multiple_of(lax.rem(zh + step + 4, 4) * R, 8), R)
        return jnp.concatenate([yown[k, rows, 0:128], yown[k, rows, 128:256]], axis=0)

    def c2(k):
        for r in range(2):
            ydir(k, r).wait_recv()
            yst(k, r).wait_recv()
            lanes = slice(r * 128, r * 128 + 128)
            yown[k, :, lanes] += ydir_r[k, r].astype(F32) + yst_r[k, r].astype(F32)
        zfar_s[k] = zrows(k, 2).astype(BF16)
        zfar(k).start()
        zdir_s[k] = zrows(k, -zway(k)).astype(BF16)
        zdir(k).start()

    def c3(k):
        zfar(k).wait_recv()
        zst_s[k] = (zrows(k, zway(k)) + zfar_r[k].astype(F32)).astype(BF16)
        zst(k).start()

    def c4(k):
        zdir(k).wait_recv()
        zst(k).wait_recv()
        done = zrows(k, 0) + (zdir_r[k].astype(F32) + zst_r[k].astype(F32))
        fin[2 * k] = done[0:R]
        fin[2 * k + 1] = done[R : 2 * R]

    def xfar(h):
        return send(xfar_s.at[h], xfar_r.at[h], xfar_ss.at[h], xfar_rs.at[h], at_x(1 - 2 * h))

    def xdir(h):
        return send(xdir_s.at[h], xdir_r.at[h], xdir_ss.at[h], xdir_rs.at[h], at_x(2 * h - 1))

    def xst(h):
        return send(xst_s.at[h], xst_r.at[h], xst_ss.at[h], xst_rs.at[h], at_x(1 - 2 * h))

    zlx = send(zl_s, zl_r, zl_ss, zl_rs, zl_peer)

    def natural():
        @pl.loop(0, T // 64)
        def _(i):
            rows = pl.ds(pl.multiple_of(i * 64, 64), 64)
            lane = lax.broadcasted_iota(jnp.int32, (64, 128), 1)

            def rolled(b):
                s = inv[b]
                block = gslot[s, rows, :].astype(F32)
                return pltpu.roll(block, 128 - 3 * b, 1) if b else block

            here = rolled(0)
            for q in range(NBLK):
                after = rolled(q + 1) if q < 15 else jnp.zeros((64, 128), F32)
                gnat[rows, q * 128 : q * 128 + 128] = jnp.where(
                    lane < BC - 3 * q, here, after
                ).astype(BF16)
                here = after

    def part_h(step, h):
        rows = pl.ds(pl.multiple_of((lax.rem(x + step, 4) * 2 + h) * RV, 16), RV)
        return h32[rows, :]

    def hm(low, high):
        @pl.loop(low, high)
        def _(j):
            cols = pl.ds(pl.multiple_of(j * 256, 256), 256)
            h32[cols, :] = dot(gnat[...], head_v[:, cols]).T

    def ha():
        natural()
        hm(0, 3)

    def h0():
        hm(3, 9)
        for h in range(2):
            xfar_s[h] = part_h(2, h).astype(BF16)
            xfar(h).start()
        xdir_s[1] = part_h(1, 1).astype(BF16)
        xdir(1).start()
        xdir_s[0] = part_h(3, 0).astype(BF16)
        xdir(0).start()

    def h1():
        xmid[0] = part_h(1, 0)
        xmid[1] = part_h(3, 1)
        for h in range(2):
            xfar(h).wait_recv()
            xst_s[h] = (xmid[h] + xfar_r[h].astype(F32)).astype(BF16)
            xst(h).start()
        for h in range(2):
            xown[h] = part_h(0, h)

    def h2():
        for h in range(2):
            xdir(h).wait_recv()
            xst(h).wait_recv()
            xown[h] += xdir_r[h].astype(F32) + xst_r[h].astype(F32)
        zl_s[...] = xown[1 - zl].astype(BF16)
        zlx.start()

    def h3():
        zlx.wait_recv()
        full = xown[zl] + zl_r[...].astype(F32)
        dhid_o[...] = full.astype(BF16)

    @pl.loop(0, TICKS)
    def _(n):
        def stage(f, lag):
            @pl.when((n >= lag) & (n < lag + NVOC))
            def _():
                f(n - lag)

        stage(c1, LAG_C1)

        @pl.when(n == 0)
        def _():
            grads(0)

        stage(mm, 0)

        @pl.when(n < 2)
        def _():
            grads(n + 1)

        @pl.when((n >= 2) & (n < 5))
        def _():
            grads(2 * n - 1)

        @pl.when((n >= 2) & (n < 4))
        def _():
            grads(2 * n)

        stage(c2, LAG_C2)
        stage(c3, LAG_C3)
        stage(c4, LAG_C4)
        pl.when(n == TICK_H)(ha)
        pl.when(n == TICK_H + 1)(h0)
        pl.when(n == TICK_H + 3)(h1)
        pl.when(n == TICK_H + 6)(h2)
        pl.when(n == TICK_H + 8)(h3)

    lane = lax.broadcasted_iota(jnp.int32, (R, 128), 1)

    def rolled_out(b):
        block = fin[inv[b]]
        return pltpu.roll(block, 128 - 3 * b, 1) if b else block

    here = rolled_out(0)
    for q in range(NBLK):
        after = rolled_out(q + 1) if q < 15 else here
        tile = jnp.where(lane < BC - 3 * q, here, after)
        if q < 15:
            dhead_o[:, q * 128 : q * 128 + 128] = tile
        else:
            dhead_o[:, 1920:V] = tile[:, 0:LAST]
        here = after

    for i in range(4):
        id_send(i).wait_send()
    for d in range(1, NVOC):
        tea_send(d).wait_send()
        tot_send(d).wait_send()
    ht_send.wait_send()

    @pl.loop(0, NVOC)
    def _(k):
        g_send(k).wait_send()
        for r in range(2):
            yfar(k, r).wait_send()
            ydir(k, r).wait_send()
            yst(k, r).wait_send()
        zfar(k).wait_send()
        zdir(k).wait_send()
        zst(k).wait_send()

    for h in range(2):
        xfar(h).wait_send()
        xdir(h).wait_send()
        xst(h).wait_send()
    zlx.wait_send()


def body(hidden, head, teacher_logp, slot_blocks, segment_ids):
    vm = pltpu.VMEM
    dma = pltpu.SemaphoreType.DMA
    chunk = (NVOC, 2)
    scratch = [
        vm((VP, T), BF16),
        vm((T, D), BF16),
        vm((VP, D), BF16),
        vm((VP, T), F32),
        vm((VP, T), F32),
        vm((NBLK, 128, T), BF16),
        vm((NVOC, 256, T), BF16),
        vm((NVOC, 256, T), BF16),
        vm((5, 8, T), jnp.int32),
        vm((D, T), F32),
        vm((D, T), BF16),
        vm((4, RY, T), BF16),
        vm((4, RY, 2 * T), BF16),
        vm((NBLK, 128, T), F32),
        vm((NBLK, 128, T), F32),
        vm((NVOC, 8, T), F32),
        vm((8, T), F32),
        vm((8, T), F32),
        vm((NVOC, 2 * T, 256), BF16),
        vm((NBLK, T, 128), BF16),
        vm((T, VP), BF16),
    ]
    scratch += [vm(chunk + (RY, 128), BF16)] * 6
    scratch += [vm(chunk + (RY, 128), F32), vm((NVOC, RY, 256), F32)]
    scratch += [vm((NVOC, 2 * R, 128), BF16)] * 6
    scratch += [vm((NBLK, R, 128), F32)]
    scratch += [vm((2, RV, T), BF16)] * 6
    scratch += [vm((2, RV, T), F32)] * 2
    scratch += [vm((RV, T), BF16)] * 2
    scratch += [pltpu.SMEM((NBLK,), jnp.int32)] * 3
    scratch += [dma((2,)), dma((4,)), dma((4,)), dma((4,)), dma((NVOC,)), dma((NVOC,)), dma(()), dma(())]
    scratch += [dma((NVOC,))] * 4
    scratch += [dma(chunk)] * 6 + [dma((NVOC,))] * 6 + [dma((2,))] * 6 + [dma(())] * 2
    anywhere = pl.BlockSpec(memory_space=pl.ANY)
    in_vmem = pl.BlockSpec(memory_space=pltpu.VMEM)
    d_hidden, d_head = pl.pallas_call(
        kernel,
        out_shape=(
            jax.ShapeDtypeStruct((RV, T), BF16),
            jax.ShapeDtypeStruct((R, V), F32),
        ),
        in_specs=[pl.BlockSpec(memory_space=pltpu.SMEM), in_vmem, anywhere, anywhere, anywhere],
        out_specs=(in_vmem, in_vmem),
        scratch_shapes=scratch,
        compiler_params=pltpu.CompilerParams(
            collective_id=0, has_side_effects=True, vmem_limit_bytes=63 * 2**20
        ),
    )(slot_blocks, segment_ids, hidden, head.T, teacher_logp.T)
    return d_hidden.T, d_head


def solution(mesh):
    placed = (P("tok", None), P(None, "voc"), P("tok", "voc"), P(), P("tok"))
    return jax.shard_map(
        body,
        mesh=mesh,
        in_specs=placed,
        out_specs=(P("tok", "voc"), P("tok", "voc")),
        check_vma=False,
    )
```

```python
import jax
import jax.numpy as jnp
from jax import lax
from jax.experimental import pallas as pl
from jax.experimental.pallas import tpu as pltpu
from jax.sharding import PartitionSpec as P

MESH = pl.DeviceIdType.MESH
F32 = jnp.float32
BF16 = jnp.bfloat16

NTOK = 32
NVOC = 8
T = 384
D = 2304
V = 2000
VP = 2048
NBLK = 16
BC = 125
LAST = V - 15 * 128
R = D // NTOK
RY = 4 * R
RV = D // NVOC
SEGS = 64
SEG_WEIGHT = 192.0
CAP = 30.0
SCALE = 1024.0

ORDER = (0, 1, 2, 7, 6, 3, 4, 5)
AHEAD = 8
LAG_C1 = 2
LAG_C2 = 3
LAG_C3 = 4
LAG_C4 = 5
TICKS = 8 + LAG_C4
TICK_H = 4


def dot(a, b):
    return jnp.dot(a, b, preferred_element_type=F32)


def dot_nt(a, b):
    return lax.dot_general(a, b, (((1,), (1,)), ((), ())), preferred_element_type=F32)


def kernel(
    slot, seg, hid_h, head_h, tea_h, dhid_o, dhead_o,
    tea_v, hid_v, head_v, tea32, nat32, tblk, tsend, trec, idb, h32, htn, hsend, ht,
    pblk, qblk, tots, arow, wrow, gc, gslot, gnat,
    yfar_s, yfar_r, ydir_s, ydir_r, yst_s, yst_r, ymid, yown,
    zfar_s, zfar_r, zdir_s, zdir_r, zst_s, zst_r, fin,
    xfar_s, xfar_r, xdir_s, xdir_r, xst_s, xst_r, xmid, xown, zl_s, zl_r,
    snd, blk, inv,
    lsem, hd_sem, id_ss, id_rs, t_ss, t_rs, ht_ss, ht_rs, tot_ss, tot_rs, g_ss, g_rs,
    yfar_ss, yfar_rs, ydir_ss, ydir_rs, yst_ss, yst_rs,
    zfar_ss, zfar_rs, zdir_ss, zdir_rs, zst_ss, zst_rs,
    xfar_ss, xfar_rs, xdir_ss, xdir_rs, xst_ss, xst_rs, zl_ss, zl_rs,
):
    t = lax.axis_index("tok")
    v = lax.axis_index("voc")
    c = lax.rem(t, 2)
    y = lax.rem(lax.div(t, 2), 4)
    zh = lax.div(t, 8)
    x = lax.div(v, 2)
    zl = lax.rem(v, 2)

    def at_y(step):
        return (zh * 8 + lax.rem(y + step + 4, 4) * 2 + c, v)

    def at_z(step):
        return (lax.rem(zh + step + 4, 4) * 8 + y * 2 + c, v)

    def at_x(step):
        return (t, lax.rem(x + step + 4, 4) * 2 + zl)

    sibling = (t + 1 - 2 * c, v)
    zl_peer = (t, v + 1 - 2 * zl)

    def at_v(step):
        return (t, lax.rem(v + step, NVOC))

    def at_t(step):
        return (lax.rem(t + step + NTOK, NTOK), v)

    def send(src, dst, ss, rs, device):
        return pltpu.make_async_remote_copy(
            src_ref=src, dst_ref=dst, send_sem=ss, recv_sem=rs, device_id=device, device_id_type=MESH
        )

    id_steps = (1, -1, 2, -2)

    barrier = pltpu.get_barrier_semaphore()
    partners = [sibling, at_y(1), at_y(-1), at_z(1), at_z(-1)]
    partners += [at_v(s) for s in range(1, NVOC)] + [at_t(s) for s in id_steps]
    for device in partners:
        pl.semaphore_signal(barrier, inc=1, device_id=device, device_id_type=MESH)

    tea_copy = pltpu.make_async_copy(tea_h, tea_v.at[pl.ds(0, V)], lsem.at[0])
    hid_copy = pltpu.make_async_copy(hid_h, hid_v, lsem.at[1])

    def head_copy(p):
        rows = pl.ds(p * 512, min(512, V - p * 512))
        return pltpu.make_async_copy(head_h.at[rows], head_v.at[rows], hd_sem.at[p])

    tea_copy.start()
    hid_copy.start()

    idb[0] = jnp.broadcast_to(seg[...].reshape(1, T), (8, T))

    tea_v[V:VP, :] = jnp.zeros((VP - V, T), BF16)
    head_v[V:VP, :] = jnp.zeros((VP - V, D), BF16)
    tea_copy.wait()
    head_copy(0).start()
    head_copy(1).start()

    def fold(values):
        return jnp.sum(values.reshape(values.shape[0] // 8, 8, T), axis=0)

    def tea_step(i, mass):
        rows = pl.ds(pl.multiple_of(i * 80, 80), 80)
        tile = tea_v[rows, :].astype(F32)
        tea32[rows, :] = tile
        return mass + fold(jnp.exp(tile))

    mass_part = lax.fori_loop(0, V // 80, tea_step, jnp.zeros((8, T), F32))
    tea32[V:VP, :] = jnp.zeros((VP - V, T), F32)

    hid_copy.wait()

    @pl.loop(0, D // 128)
    def _(j):
        off = pl.multiple_of(j * 128, 128)
        turned = hid_v[:, pl.ds(off, 128)].astype(F32).T
        h32[pl.ds(off, 128), :] = turned
        htn[pl.ds(off, 128), :] = turned.astype(BF16)

    total_part = jnp.zeros((8, T), F32)
    valid = lax.broadcasted_iota(jnp.int32, (128, T), 0) < BC
    for p in range(5):
        if p < 4:
            head_copy(p).wait()
            if p < 2:
                head_copy(p + 2).start()
            nat32[p * 512 : p * 512 + 512, :] = dot(head_v[p * 512 : p * 512 + 512, :], htn[...])
        for b in range(4 * p - 4, 4 * p):
            if b < 0:
                continue
            th = jnp.tanh(nat32[b * BC : b * BC + 128, :] * (1.0 / CAP))
            shifted = jnp.exp(CAP * th - CAP)
            slope = 1.0 - th * th
            pblk[b] = shifted * slope
            qblk[b] = slope
            total_part += fold(jnp.where(valid, shifted, 0.0))

    sub = lax.broadcasted_iota(jnp.int32, (8, T), 0)
    total_row = jnp.sum(total_part, axis=0, keepdims=True)
    mass_row = jnp.sum(mass_part, axis=0, keepdims=True)
    tots[0] = jnp.where(sub == 0, total_row, mass_row)

    def tot_send(d):
        return send(tots.at[0], tots.at[NVOC - d], tot_ss.at[d], tot_rs.at[NVOC - d], at_v(d))

    pl.semaphore_wait(barrier, len(partners))
    for d in range(1, NVOC):
        tot_send(d).start()

    def tea_send(k):
        back = NVOC - (ORDER[k] if isinstance(k, int) else offset(k))
        return send(tsend.at[k], trec.at[k], t_ss.at[k], t_rs.at[k], at_v(back))

    def id_send(i):
        return send(idb.at[0], idb.at[i + 1], id_ss.at[i], id_rs.at[i], at_t(id_steps[i]))

    for i in range(4):
        id_send(i).start()

    def pack(core, yy):
        parts = []
        for z in range(4):
            parts.append(h32[pl.ds(pl.multiple_of((8 * z + 2 * yy + core) * R, 8), R), :])
        return jnp.concatenate(parts, axis=0).astype(BF16)

    @pl.loop(0, 4)
    def _(yy):
        hsend[yy] = pack(1 - c, yy)

    ht_send = send(hsend, ht.at[:, :, pl.ds(T, T)], ht_ss, ht_rs, sibling)
    ht_send.start()

    @pl.loop(0, 4)
    def _(yy):
        ht[yy, :, 0:T] = pack(c, yy)

    def offset(k):
        out = jnp.int32(0)
        for i in range(1, NVOC):
            out = jnp.where(k == i, ORDER[i], out)
        return out

    @pl.loop(0, NVOC)
    def _(d):
        low = lax.rem(v + NVOC - offset(d), NVOC) * NBLK
        first = jnp.int32(0)
        last = jnp.int32(0)
        for j in range(NBLK):
            e = slot[v * NBLK + j]
            last = jnp.where((e >= low) & (e < low + NBLK), j, last)
            e = slot[v * NBLK + NBLK - 1 - j]
            first = jnp.where((e >= low) & (e < low + NBLK), NBLK - 1 - j, first)
        snd[2 * d] = first
        snd[2 * d + 1] = last

    for b in range(NBLK):
        tblk[b] = tea32[b * BC : b * BC + 128, :].astype(BF16)

    for d in range(NVOC):
        for r in range(2):
            target = trec.at[0] if d == 0 else tsend.at[d]
            target[r * 128 : r * 128 + 128, :] = tblk[snd[2 * d + r]]

    for k in range(1, AHEAD):
        tea_send(k).start()

    @pl.loop(0, NVOC)
    def _(k):
        base = lax.rem(v + offset(k), NVOC) * NBLK
        low = v * NBLK
        first = jnp.int32(0)
        last = jnp.int32(0)
        for j in range(NBLK):
            e = slot[base + j]
            last = jnp.where((e >= low) & (e < low + NBLK), e - low, last)
            e = slot[base + NBLK - 1 - j]
            first = jnp.where((e >= low) & (e < low + NBLK), e - low, first)
        blk[2 * k] = first
        blk[2 * k + 1] = last

    @pl.loop(0, NBLK)
    def _(b):
        place = jnp.int32(0)
        for s in range(NBLK):
            place = jnp.where(blk[s] == b, s, place)
        inv[b] = place

    for i in range(4):
        id_send(i).wait_recv()
    segments = lax.broadcasted_iota(jnp.int32, (SEGS, T), 0)
    own_hit = segments == idb[0, 0:1, :]
    hits = own_hit.astype(F32)
    for i in range(1, 5):
        hits += (segments == idb[i, 0:1, :]).astype(F32)
    counts = jnp.sum(hits, axis=1, keepdims=True)
    seg_size = jnp.sum(jnp.where(own_hit, counts, 0.0), axis=0, keepdims=True)
    weight = (SCALE * SEG_WEIGHT) / seg_size
    wrow[...] = jnp.broadcast_to(weight, (8, T))

    for d in range(1, NVOC):
        tot_send(NVOC - d).wait_recv()
    sums = tots[0]
    for d in range(1, NVOC):
        sums += tots[d]
    ratio = weight * (sums[1:2, :] / sums[0:1, :])
    arow[...] = jnp.broadcast_to(ratio, (8, T))

    for k in range(AHEAD, NVOC):
        tea_send(k).start()
    ht_send.wait_recv()

    def g_send(k):
        return send(
            gc.at[k, pl.ds(0, T), :], gc.at[k, pl.ds(T, T), :], g_ss.at[k], g_rs.at[k], sibling
        )

    def yfar(k, r):
        return send(yfar_s.at[k, r], yfar_r.at[k, r], yfar_ss.at[k, r], yfar_rs.at[k, r], at_y(1 - 2 * r))

    def ydir(k, r):
        return send(ydir_s.at[k, r], ydir_r.at[k, r], ydir_ss.at[k, r], ydir_rs.at[k, r], at_y(2 * r - 1))

    def yst(k, r):
        return send(yst_s.at[k, r], yst_r.at[k, r], yst_ss.at[k, r], yst_rs.at[k, r], at_y(1 - 2 * r))

    def zway(k):
        return 1 - 2 * lax.rem(k, 2)

    def zfar(k):
        return send(zfar_s.at[k], zfar_r.at[k], zfar_ss.at[k], zfar_rs.at[k], at_z(zway(k)))

    def zdir(k):
        return send(zdir_s.at[k], zdir_r.at[k], zdir_ss.at[k], zdir_rs.at[k], at_z(-zway(k)))

    def zst(k):
        return send(zst_s.at[k], zst_r.at[k], zst_ss.at[k], zst_rs.at[k], at_z(zway(k)))

    def grads(k):
        @pl.when(k > 0)
        def _():
            tea_send(k).wait_recv()

        for r in range(2):
            b = blk[2 * k + r]
            prob = jnp.exp(trec[k, r * 128 : r * 128 + 128, :].astype(F32))
            grad = arow[0:1, :] * pblk[b] - wrow[0:1, :] * (prob * qblk[b])
            grad = grad.T.astype(BF16)
            gc[k, 0:T, r * 128 : r * 128 + 128] = grad
            gslot[2 * k + r] = grad

        g_send(k).start()

    def mm(k):
        g_send(k).wait_recv()
        far = dot(ht[lax.rem(y + 2, 4)], gc[k])
        for r in range(2):
            yfar_s[k, r] = far[:, r * 128 : r * 128 + 128].astype(BF16)
            yfar(k, r).start()
        part = dot(ht[lax.rem(y + 1, 4)], gc[k])
        ydir_s[k, 1] = part[:, 128:].astype(BF16)
        ydir(k, 1).start()
        ymid[k, 0] = part[:, :128]
        part = dot(ht[lax.rem(y + 3, 4)], gc[k])
        ydir_s[k, 0] = part[:, :128].astype(BF16)
        ydir(k, 0).start()
        ymid[k, 1] = part[:, 128:]
        yown[k] = dot(ht[y], gc[k])

    def c1(k):
        for r in range(2):
            yfar(k, r).wait_recv()
            yst_s[k, r] = (ymid[k, r] + yfar_r[k, r].astype(F32)).astype(BF16)
            yst(k, r).start()

    def zrows(k, step):
        rows = pl.ds(pl.multiple_of(lax.rem(zh + step + 4, 4) * R, 8), R)
        return jnp.concatenate([yown[k, rows, 0:128], yown[k, rows, 128:256]], axis=0)

    def c2(k):
        for r in range(2):
            ydir(k, r).wait_recv()
            yst(k, r).wait_recv()
            lanes = slice(r * 128, r * 128 + 128)
            yown[k, :, lanes] += ydir_r[k, r].astype(F32) + yst_r[k, r].astype(F32)
        zfar_s[k] = zrows(k, 2).astype(BF16)
        zfar(k).start()
        zdir_s[k] = zrows(k, -zway(k)).astype(BF16)
        zdir(k).start()

    def c3(k):
        zfar(k).wait_recv()
        zst_s[k] = (zrows(k, zway(k)) + zfar_r[k].astype(F32)).astype(BF16)
        zst(k).start()

    def c4(k):
        zdir(k).wait_recv()
        zst(k).wait_recv()
        done = zrows(k, 0) + (zdir_r[k].astype(F32) + zst_r[k].astype(F32))
        fin[2 * k] = done[0:R]
        fin[2 * k + 1] = done[R : 2 * R]

    def xfar(h):
        return send(xfar_s.at[h], xfar_r.at[h], xfar_ss.at[h], xfar_rs.at[h], at_x(1 - 2 * h))

    def xdir(h):
        return send(xdir_s.at[h], xdir_r.at[h], xdir_ss.at[h], xdir_rs.at[h], at_x(2 * h - 1))

    def xst(h):
        return send(xst_s.at[h], xst_r.at[h], xst_ss.at[h], xst_rs.at[h], at_x(1 - 2 * h))

    zlx = send(zl_s, zl_r, zl_ss, zl_rs, zl_peer)

    def natural():
        @pl.loop(0, T // 64)
        def _(i):
            rows = pl.ds(pl.multiple_of(i * 64, 64), 64)
            lane = lax.broadcasted_iota(jnp.int32, (64, 128), 1)

            def rolled(b):
                s = inv[b]
                block = gslot[s, rows, :].astype(F32)
                return pltpu.roll(block, 128 - 3 * b, 1) if b else block

            here = rolled(0)
            for q in range(NBLK):
                after = rolled(q + 1) if q < 15 else jnp.zeros((64, 128), F32)
                gnat[rows, q * 128 : q * 128 + 128] = jnp.where(
                    lane < BC - 3 * q, here, after
                ).astype(BF16)
                here = after

    def part_h(step, h):
        rows = pl.ds(pl.multiple_of((lax.rem(x + step, 4) * 2 + h) * RV, 16), RV)
        return h32[rows, :]

    def hm(low, high):
        @pl.loop(low, high)
        def _(j):
            cols = pl.ds(pl.multiple_of(j * 256, 256), 256)
            h32[cols, :] = dot(gnat[...], head_v[:, cols]).T

    def ha():
        natural()
        hm(0, 3)

    def h0():
        hm(6, 9)
        for h in range(2):
            xfar_s[h] = part_h(2, h).astype(BF16)
            xfar(h).start()

    def hd():
        xdir_s[1] = part_h(1, 1).astype(BF16)
        xdir(1).start()
        xdir_s[0] = part_h(3, 0).astype(BF16)
        xdir(0).start()

    def h1():
        xmid[0] = part_h(1, 0)
        xmid[1] = part_h(3, 1)
        for h in range(2):
            xfar(h).wait_recv()
            xst_s[h] = (xmid[h] + xfar_r[h].astype(F32)).astype(BF16)
            xst(h).start()
        for h in range(2):
            xown[h] = part_h(0, h)

    def h2():
        for h in range(2):
            xdir(h).wait_recv()
            xst(h).wait_recv()
            xown[h] += xdir_r[h].astype(F32) + xst_r[h].astype(F32)
        zl_s[...] = xown[1 - zl].astype(BF16)
        zlx.start()

    def h3():
        zlx.wait_recv()
        full = xown[zl] + zl_r[...].astype(F32)
        dhid_o[...] = full.astype(BF16)

    @pl.loop(0, TICKS)
    def _(n):
        def stage(f, lag):
            @pl.when((n >= lag) & (n < lag + NVOC))
            def _():
                f(n - lag)

        stage(c1, LAG_C1)

        @pl.when(n == 0)
        def _():
            grads(0)

        stage(mm, 0)

        @pl.when(n < 2)
        def _():
            grads(n + 1)

        @pl.when((n >= 2) & (n < 5))
        def _():
            grads(2 * n - 1)

        @pl.when((n >= 2) & (n < 4))
        def _():
            grads(2 * n)

        stage(c2, LAG_C2)
        stage(c3, LAG_C3)
        stage(c4, LAG_C4)
        pl.when(n == TICK_H)(ha)
        pl.when(n == TICK_H + 1)(lambda: hm(3, 6))
        pl.when(n == TICK_H + 2)(h0)
        pl.when(n == TICK_H + 3)(hd)
        pl.when(n == TICK_H + 3)(h1)
        pl.when(n == TICK_H + 6)(h2)
        pl.when(n == TICK_H + 8)(h3)

    lane = lax.broadcasted_iota(jnp.int32, (R, 128), 1)

    def rolled_out(b):
        block = fin[inv[b]]
        return pltpu.roll(block, 128 - 3 * b, 1) if b else block

    here = rolled_out(0)
    for q in range(NBLK):
        after = rolled_out(q + 1) if q < 15 else here
        tile = jnp.where(lane < BC - 3 * q, here, after)
        if q < 15:
            dhead_o[:, q * 128 : q * 128 + 128] = tile
        else:
            dhead_o[:, 1920:V] = tile[:, 0:LAST]
        here = after

    for i in range(4):
        id_send(i).wait_send()
    for d in range(1, NVOC):
        tea_send(d).wait_send()
        tot_send(d).wait_send()
    ht_send.wait_send()

    @pl.loop(0, NVOC)
    def _(k):
        g_send(k).wait_send()
        for r in range(2):
            yfar(k, r).wait_send()
            ydir(k, r).wait_send()
            yst(k, r).wait_send()
        zfar(k).wait_send()
        zdir(k).wait_send()
        zst(k).wait_send()

    for h in range(2):
        xfar(h).wait_send()
        xdir(h).wait_send()
        xst(h).wait_send()
    zlx.wait_send()


def body(hidden, head, teacher_logp, slot_blocks, segment_ids):
    vm = pltpu.VMEM
    dma = pltpu.SemaphoreType.DMA
    chunk = (NVOC, 2)
    scratch = [
        vm((VP, T), BF16),
        vm((T, D), BF16),
        vm((VP, D), BF16),
        vm((VP, T), F32),
        vm((VP, T), F32),
        vm((NBLK, 128, T), BF16),
        vm((NVOC, 256, T), BF16),
        vm((NVOC, 256, T), BF16),
        vm((5, 8, T), jnp.int32),
        vm((D, T), F32),
        vm((D, T), BF16),
        vm((4, RY, T), BF16),
        vm((4, RY, 2 * T), BF16),
        vm((NBLK, 128, T), F32),
        vm((NBLK, 128, T), F32),
        vm((NVOC, 8, T), F32),
        vm((8, T), F32),
        vm((8, T), F32),
        vm((NVOC, 2 * T, 256), BF16),
        vm((NBLK, T, 128), BF16),
        vm((T, VP), BF16),
    ]
    scratch += [vm(chunk + (RY, 128), BF16)] * 6
    scratch += [vm(chunk + (RY, 128), F32), vm((NVOC, RY, 256), F32)]
    scratch += [vm((NVOC, 2 * R, 128), BF16)] * 6
    scratch += [vm((NBLK, R, 128), F32)]
    scratch += [vm((2, RV, T), BF16)] * 6
    scratch += [vm((2, RV, T), F32)] * 2
    scratch += [vm((RV, T), BF16)] * 2
    scratch += [pltpu.SMEM((NBLK,), jnp.int32)] * 3
    scratch += [dma((2,)), dma((4,)), dma((4,)), dma((4,)), dma((NVOC,)), dma((NVOC,)), dma(()), dma(())]
    scratch += [dma((NVOC,))] * 4
    scratch += [dma(chunk)] * 6 + [dma((NVOC,))] * 6 + [dma((2,))] * 6 + [dma(())] * 2
    anywhere = pl.BlockSpec(memory_space=pl.ANY)
    in_vmem = pl.BlockSpec(memory_space=pltpu.VMEM)
    d_hidden, d_head = pl.pallas_call(
        kernel,
        out_shape=(
            jax.ShapeDtypeStruct((RV, T), BF16),
            jax.ShapeDtypeStruct((R, V), F32),
        ),
        in_specs=[pl.BlockSpec(memory_space=pltpu.SMEM), in_vmem, anywhere, anywhere, anywhere],
        out_specs=(in_vmem, in_vmem),
        scratch_shapes=scratch,
        compiler_params=pltpu.CompilerParams(
            collective_id=0, has_side_effects=True, vmem_limit_bytes=63 * 2**20
        ),
    )(slot_blocks, segment_ids, hidden, head.T, teacher_logp.T)
    return d_hidden.T, d_head


def solution(mesh):
    placed = (P("tok", None), P(None, "voc"), P("tok", "voc"), P(), P("tok"))
    return jax.shard_map(
        body,
        mesh=mesh,
        in_specs=placed,
        out_specs=(P("tok", "voc"), P("tok", "voc")),
        check_vma=False,
    )
```

```python
import jax
import jax.numpy as jnp
from jax import lax
from jax.experimental import pallas as pl
from jax.experimental.pallas import tpu as pltpu
from jax.sharding import PartitionSpec as P

MESH = pl.DeviceIdType.MESH
F32 = jnp.float32
BF16 = jnp.bfloat16

NTOK = 32
NVOC = 8
T = 384
D = 2304
V = 2000
VP = 2048
NBLK = 16
BC = 125
LAST = V - 15 * 128
R = D // NTOK
RY = 4 * R
RV = D // NVOC
SEGS = 64
SEG_WEIGHT = 192.0
CAP = 30.0
SCALE = 1024.0

ORDER = (0, 1, 2, 7, 6, 3, 4, 5)
AHEAD = 8
LAG_C1 = 2
LAG_C2 = 3
LAG_C3 = 4
LAG_C4 = 5
TICKS = 8 + LAG_C4
TICK_H = 4


def dot(a, b):
    return jnp.dot(a, b, preferred_element_type=F32)


def dot_nt(a, b):
    return lax.dot_general(a, b, (((1,), (1,)), ((), ())), preferred_element_type=F32)


def kernel(
    slot, seg, hid_h, head_h, tea_h, dhid_o, fin, inv,
    tea_v, hid_v, head_v, tea32, nat32, tblk, tsend, trec, idb, h32, htn, hsend, ht,
    pblk, qblk, tots, arow, wrow, gc, gslot, gnat,
    yfar_s, yfar_r, ydir_s, ydir_r, yst_s, yst_r, ymid, yown,
    zfar_s, zfar_r, zdir_s, zdir_r, zst_s, zst_r,
    xfar_s, xfar_r, xdir_s, xdir_r, xst_s, xst_r, xmid, xown, zl_s, zl_r,
    snd, blk,
    lsem, hd_sem, id_ss, id_rs, t_ss, t_rs, ht_ss, ht_rs, tot_ss, tot_rs, g_ss, g_rs,
    yfar_ss, yfar_rs, ydir_ss, ydir_rs, yst_ss, yst_rs,
    zfar_ss, zfar_rs, zdir_ss, zdir_rs, zst_ss, zst_rs,
    xfar_ss, xfar_rs, xdir_ss, xdir_rs, xst_ss, xst_rs, zl_ss, zl_rs,
):
    t = lax.axis_index("tok")
    v = lax.axis_index("voc")
    c = lax.rem(t, 2)
    y = lax.rem(lax.div(t, 2), 4)
    zh = lax.div(t, 8)
    x = lax.div(v, 2)
    zl = lax.rem(v, 2)

    def at_y(step):
        return (zh * 8 + lax.rem(y + step + 4, 4) * 2 + c, v)

    def at_z(step):
        return (lax.rem(zh + step + 4, 4) * 8 + y * 2 + c, v)

    def at_x(step):
        return (t, lax.rem(x + step + 4, 4) * 2 + zl)

    sibling = (t + 1 - 2 * c, v)
    zl_peer = (t, v + 1 - 2 * zl)

    def at_v(step):
        return (t, lax.rem(v + step, NVOC))

    def at_t(step):
        return (lax.rem(t + step + NTOK, NTOK), v)

    def send(src, dst, ss, rs, device):
        return pltpu.make_async_remote_copy(
            src_ref=src, dst_ref=dst, send_sem=ss, recv_sem=rs, device_id=device, device_id_type=MESH
        )

    id_steps = (1, -1, 2, -2)

    barrier = pltpu.get_barrier_semaphore()
    partners = [sibling, at_y(1), at_y(-1), at_z(1), at_z(-1)]
    partners += [at_v(s) for s in range(1, NVOC)] + [at_t(s) for s in id_steps]
    for device in partners:
        pl.semaphore_signal(barrier, inc=1, device_id=device, device_id_type=MESH)

    tea_copy = pltpu.make_async_copy(tea_h, tea_v.at[pl.ds(0, V)], lsem.at[0])
    hid_copy = pltpu.make_async_copy(hid_h, hid_v, lsem.at[1])

    def head_copy(p):
        rows = pl.ds(p * 512, min(512, V - p * 512))
        return pltpu.make_async_copy(head_h.at[rows], head_v.at[rows], hd_sem.at[p])

    tea_copy.start()
    hid_copy.start()

    idb[0] = jnp.broadcast_to(seg[...].reshape(1, T), (8, T))

    tea_v[V:VP, :] = jnp.zeros((VP - V, T), BF16)
    head_v[V:VP, :] = jnp.zeros((VP - V, D), BF16)
    tea_copy.wait()
    head_copy(0).start()
    head_copy(1).start()

    def fold(values):
        return jnp.sum(values.reshape(values.shape[0] // 8, 8, T), axis=0)

    def tea_step(i, mass):
        rows = pl.ds(pl.multiple_of(i * 80, 80), 80)
        tile = tea_v[rows, :].astype(F32)
        tea32[rows, :] = tile
        return mass + fold(jnp.exp(tile))

    mass_part = lax.fori_loop(0, V // 80, tea_step, jnp.zeros((8, T), F32))
    tea32[V:VP, :] = jnp.zeros((VP - V, T), F32)

    hid_copy.wait()

    @pl.loop(0, D // 128)
    def _(j):
        off = pl.multiple_of(j * 128, 128)
        turned = hid_v[:, pl.ds(off, 128)].astype(F32).T
        h32[pl.ds(off, 128), :] = turned
        htn[pl.ds(off, 128), :] = turned.astype(BF16)

    total_part = jnp.zeros((8, T), F32)
    valid = lax.broadcasted_iota(jnp.int32, (128, T), 0) < BC
    for p in range(5):
        if p < 4:
            head_copy(p).wait()
            if p < 2:
                head_copy(p + 2).start()
            nat32[p * 512 : p * 512 + 512, :] = dot(head_v[p * 512 : p * 512 + 512, :], htn[...])
        for b in range(4 * p - 4, 4 * p):
            if b < 0:
                continue
            th = jnp.tanh(nat32[b * BC : b * BC + 128, :] * (1.0 / CAP))
            shifted = jnp.exp(CAP * th - CAP)
            slope = 1.0 - th * th
            pblk[b] = shifted * slope
            qblk[b] = slope
            total_part += fold(jnp.where(valid, shifted, 0.0))

    sub = lax.broadcasted_iota(jnp.int32, (8, T), 0)
    total_row = jnp.sum(total_part, axis=0, keepdims=True)
    mass_row = jnp.sum(mass_part, axis=0, keepdims=True)
    tots[0] = jnp.where(sub == 0, total_row, mass_row)

    def tot_send(d):
        return send(tots.at[0], tots.at[NVOC - d], tot_ss.at[d], tot_rs.at[NVOC - d], at_v(d))

    pl.semaphore_wait(barrier, len(partners))
    for d in range(1, NVOC):
        tot_send(d).start()

    def tea_send(k):
        back = NVOC - (ORDER[k] if isinstance(k, int) else offset(k))
        return send(tsend.at[k], trec.at[k], t_ss.at[k], t_rs.at[k], at_v(back))

    def id_send(i):
        return send(idb.at[0], idb.at[i + 1], id_ss.at[i], id_rs.at[i], at_t(id_steps[i]))

    for i in range(4):
        id_send(i).start()

    def pack(core, yy):
        parts = []
        for z in range(4):
            parts.append(h32[pl.ds(pl.multiple_of((8 * z + 2 * yy + core) * R, 8), R), :])
        return jnp.concatenate(parts, axis=0).astype(BF16)

    @pl.loop(0, 4)
    def _(yy):
        hsend[yy] = pack(1 - c, yy)

    ht_send = send(hsend, ht.at[:, :, pl.ds(T, T)], ht_ss, ht_rs, sibling)
    ht_send.start()

    @pl.loop(0, 4)
    def _(yy):
        ht[yy, :, 0:T] = pack(c, yy)

    def offset(k):
        out = jnp.int32(0)
        for i in range(1, NVOC):
            out = jnp.where(k == i, ORDER[i], out)
        return out

    @pl.loop(0, NVOC)
    def _(d):
        low = lax.rem(v + NVOC - offset(d), NVOC) * NBLK
        first = jnp.int32(0)
        last = jnp.int32(0)
        for j in range(NBLK):
            e = slot[v * NBLK + j]
            last = jnp.where((e >= low) & (e < low + NBLK), j, last)
            e = slot[v * NBLK + NBLK - 1 - j]
            first = jnp.where((e >= low) & (e < low + NBLK), NBLK - 1 - j, first)
        snd[2 * d] = first
        snd[2 * d + 1] = last

    for b in range(NBLK):
        tblk[b] = tea32[b * BC : b * BC + 128, :].astype(BF16)

    for d in range(NVOC):
        for r in range(2):
            target = trec.at[0] if d == 0 else tsend.at[d]
            target[r * 128 : r * 128 + 128, :] = tblk[snd[2 * d + r]]

    for k in range(1, AHEAD):
        tea_send(k).start()

    @pl.loop(0, NVOC)
    def _(k):
        base = lax.rem(v + offset(k), NVOC) * NBLK
        low = v * NBLK
        first = jnp.int32(0)
        last = jnp.int32(0)
        for j in range(NBLK):
            e = slot[base + j]
            last = jnp.where((e >= low) & (e < low + NBLK), e - low, last)
            e = slot[base + NBLK - 1 - j]
            first = jnp.where((e >= low) & (e < low + NBLK), e - low, first)
        blk[2 * k] = first
        blk[2 * k + 1] = last

    @pl.loop(0, NBLK)
    def _(b):
        place = jnp.int32(0)
        for s in range(NBLK):
            place = jnp.where(blk[s] == b, s, place)
        inv[b] = place

    for i in range(4):
        id_send(i).wait_recv()
    segments = lax.broadcasted_iota(jnp.int32, (SEGS, T), 0)
    own_hit = segments == idb[0, 0:1, :]
    hits = own_hit.astype(F32)
    for i in range(1, 5):
        hits += (segments == idb[i, 0:1, :]).astype(F32)
    counts = jnp.sum(hits, axis=1, keepdims=True)
    seg_size = jnp.sum(jnp.where(own_hit, counts, 0.0), axis=0, keepdims=True)
    weight = (SCALE * SEG_WEIGHT) / seg_size
    wrow[...] = jnp.broadcast_to(weight, (8, T))

    for d in range(1, NVOC):
        tot_send(NVOC - d).wait_recv()
    sums = tots[0]
    for d in range(1, NVOC):
        sums += tots[d]
    ratio = weight * (sums[1:2, :] / sums[0:1, :])
    arow[...] = jnp.broadcast_to(ratio, (8, T))

    for k in range(AHEAD, NVOC):
        tea_send(k).start()
    ht_send.wait_recv()

    def g_send(k):
        return send(
            gc.at[k, pl.ds(0, T), :], gc.at[k, pl.ds(T, T), :], g_ss.at[k], g_rs.at[k], sibling
        )

    def yfar(k, r):
        return send(yfar_s.at[k, r], yfar_r.at[k, r], yfar_ss.at[k, r], yfar_rs.at[k, r], at_y(1 - 2 * r))

    def ydir(k, r):
        return send(ydir_s.at[k, r], ydir_r.at[k, r], ydir_ss.at[k, r], ydir_rs.at[k, r], at_y(2 * r - 1))

    def yst(k, r):
        return send(yst_s.at[k, r], yst_r.at[k, r], yst_ss.at[k, r], yst_rs.at[k, r], at_y(1 - 2 * r))

    def zway(k):
        return 1 - 2 * lax.rem(k, 2)

    def zfar(k):
        return send(zfar_s.at[k], zfar_r.at[k], zfar_ss.at[k], zfar_rs.at[k], at_z(zway(k)))

    def zdir(k):
        return send(zdir_s.at[k], zdir_r.at[k], zdir_ss.at[k], zdir_rs.at[k], at_z(-zway(k)))

    def zst(k):
        return send(zst_s.at[k], zst_r.at[k], zst_ss.at[k], zst_rs.at[k], at_z(zway(k)))

    def grads(k):
        @pl.when(k > 0)
        def _():
            tea_send(k).wait_recv()

        for r in range(2):
            b = blk[2 * k + r]
            prob = jnp.exp(trec[k, r * 128 : r * 128 + 128, :].astype(F32))
            grad = arow[0:1, :] * pblk[b] - wrow[0:1, :] * (prob * qblk[b])
            grad = grad.T.astype(BF16)
            gc[k, 0:T, r * 128 : r * 128 + 128] = grad
            gslot[2 * k + r] = grad

        g_send(k).start()

    def mm(k):
        g_send(k).wait_recv()
        far = dot(ht[lax.rem(y + 2, 4)], gc[k])
        for r in range(2):
            yfar_s[k, r] = far[:, r * 128 : r * 128 + 128].astype(BF16)
            yfar(k, r).start()
        part = dot(ht[lax.rem(y + 1, 4)], gc[k])
        ydir_s[k, 1] = part[:, 128:].astype(BF16)
        ydir(k, 1).start()
        ymid[k, 0] = part[:, :128]
        part = dot(ht[lax.rem(y + 3, 4)], gc[k])
        ydir_s[k, 0] = part[:, :128].astype(BF16)
        ydir(k, 0).start()
        ymid[k, 1] = part[:, 128:]
        yown[k] = dot(ht[y], gc[k])

    def c1(k):
        for r in range(2):
            yfar(k, r).wait_recv()
            yst_s[k, r] = (ymid[k, r] + yfar_r[k, r].astype(F32)).astype(BF16)
            yst(k, r).start()

    def zrows(k, step):
        rows = pl.ds(pl.multiple_of(lax.rem(zh + step + 4, 4) * R, 8), R)
        return jnp.concatenate([yown[k, rows, 0:128], yown[k, rows, 128:256]], axis=0)

    def c2(k):
        for r in range(2):
            ydir(k, r).wait_recv()
            yst(k, r).wait_recv()
            lanes = slice(r * 128, r * 128 + 128)
            yown[k, :, lanes] += ydir_r[k, r].astype(F32) + yst_r[k, r].astype(F32)
        zfar_s[k] = zrows(k, 2).astype(BF16)
        zfar(k).start()
        zdir_s[k] = zrows(k, -zway(k)).astype(BF16)
        zdir(k).start()

    def c3(k):
        zfar(k).wait_recv()
        zst_s[k] = (zrows(k, zway(k)) + zfar_r[k].astype(F32)).astype(BF16)
        zst(k).start()

    def c4(k):
        zdir(k).wait_recv()
        zst(k).wait_recv()
        done = zrows(k, 0) + (zdir_r[k].astype(F32) + zst_r[k].astype(F32))
        fin[2 * k] = done[0:R]
        fin[2 * k + 1] = done[R : 2 * R]

    def xfar(h):
        return send(xfar_s.at[h], xfar_r.at[h], xfar_ss.at[h], xfar_rs.at[h], at_x(1 - 2 * h))

    def xdir(h):
        return send(xdir_s.at[h], xdir_r.at[h], xdir_ss.at[h], xdir_rs.at[h], at_x(2 * h - 1))

    def xst(h):
        return send(xst_s.at[h], xst_r.at[h], xst_ss.at[h], xst_rs.at[h], at_x(1 - 2 * h))

    zlx = send(zl_s, zl_r, zl_ss, zl_rs, zl_peer)

    def natural():
        @pl.loop(0, T // 64)
        def _(i):
            rows = pl.ds(pl.multiple_of(i * 64, 64), 64)
            lane = lax.broadcasted_iota(jnp.int32, (64, 128), 1)

            def rolled(b):
                s = inv[b]
                block = gslot[s, rows, :].astype(F32)
                return pltpu.roll(block, 128 - 3 * b, 1) if b else block

            here = rolled(0)
            for q in range(NBLK):
                after = rolled(q + 1) if q < 15 else jnp.zeros((64, 128), F32)
                gnat[rows, q * 128 : q * 128 + 128] = jnp.where(
                    lane < BC - 3 * q, here, after
                ).astype(BF16)
                here = after

    def part_h(step, h):
        rows = pl.ds(pl.multiple_of((lax.rem(x + step, 4) * 2 + h) * RV, 16), RV)
        return h32[rows, :]

    def hm(low, high):
        @pl.loop(low, high)
        def _(j):
            cols = pl.ds(pl.multiple_of(j * 256, 256), 256)
            h32[cols, :] = dot(gnat[...], head_v[:, cols]).T

    def ha():
        natural()
        hm(0, 3)

    def h0():
        hm(6, 9)
        for h in range(2):
            xfar_s[h] = part_h(2, h).astype(BF16)
            xfar(h).start()

    def hd():
        xdir_s[1] = part_h(1, 1).astype(BF16)
        xdir(1).start()
        xdir_s[0] = part_h(3, 0).astype(BF16)
        xdir(0).start()

    def h1():
        xmid[0] = part_h(1, 0)
        xmid[1] = part_h(3, 1)
        for h in range(2):
            xfar(h).wait_recv()
            xst_s[h] = (xmid[h] + xfar_r[h].astype(F32)).astype(BF16)
            xst(h).start()
        for h in range(2):
            xown[h] = part_h(0, h)

    def h2():
        for h in range(2):
            xdir(h).wait_recv()
            xst(h).wait_recv()
            xown[h] += xdir_r[h].astype(F32) + xst_r[h].astype(F32)
        zl_s[...] = xown[1 - zl].astype(BF16)
        zlx.start()

    def h3():
        zlx.wait_recv()
        full = xown[zl] + zl_r[...].astype(F32)
        dhid_o[...] = full.astype(BF16)

    @pl.loop(0, TICKS)
    def _(n):
        def stage(f, lag):
            @pl.when((n >= lag) & (n < lag + NVOC))
            def _():
                f(n - lag)

        stage(c1, LAG_C1)

        @pl.when(n == 0)
        def _():
            grads(0)

        stage(mm, 0)

        @pl.when(n < 2)
        def _():
            grads(n + 1)

        @pl.when((n >= 2) & (n < 5))
        def _():
            grads(2 * n - 1)

        @pl.when((n >= 2) & (n < 4))
        def _():
            grads(2 * n)

        stage(c2, LAG_C2)
        stage(c3, LAG_C3)
        stage(c4, LAG_C4)
        pl.when(n == TICK_H)(ha)
        pl.when(n == TICK_H + 1)(lambda: hm(3, 6))
        pl.when(n == TICK_H + 2)(h0)
        pl.when(n == TICK_H + 3)(hd)
        pl.when(n == TICK_H + 3)(h1)
        pl.when(n == TICK_H + 6)(h2)
        pl.when(n == TICK_H + 8)(h3)

    for i in range(4):
        id_send(i).wait_send()
    for d in range(1, NVOC):
        tea_send(d).wait_send()
        tot_send(d).wait_send()
    ht_send.wait_send()

    @pl.loop(0, NVOC)
    def _(k):
        g_send(k).wait_send()
        for r in range(2):
            yfar(k, r).wait_send()
            ydir(k, r).wait_send()
            yst(k, r).wait_send()
        zfar(k).wait_send()
        zdir(k).wait_send()
        zst(k).wait_send()

    for h in range(2):
        xfar(h).wait_send()
        xdir(h).wait_send()
        xst(h).wait_send()
    zlx.wait_send()


def finish(inv, fin, dhid, dhid_o, dhead_o):
    lane = lax.broadcasted_iota(jnp.int32, (R, 128), 1)

    def rolled_out(b):
        block = fin[inv[b]]
        return pltpu.roll(block, 128 - 3 * b, 1) if b else block

    here = rolled_out(0)
    for q in range(NBLK):
        after = rolled_out(q + 1) if q < 15 else here
        tile = jnp.where(lane < BC - 3 * q, here, after)
        if q < 15:
            dhead_o[:, q * 128 : q * 128 + 128] = tile
        else:
            dhead_o[:, 1920:V] = tile[:, 0:LAST]
        here = after
    dhid_o[...] = dhid[...]


def body(hidden, head, teacher_logp, slot_blocks, segment_ids):
    vm = pltpu.VMEM
    dma = pltpu.SemaphoreType.DMA
    chunk = (NVOC, 2)
    scratch = [
        vm((VP, T), BF16),
        vm((T, D), BF16),
        vm((VP, D), BF16),
        vm((VP, T), F32),
        vm((VP, T), F32),
        vm((NBLK, 128, T), BF16),
        vm((NVOC, 256, T), BF16),
        vm((NVOC, 256, T), BF16),
        vm((5, 8, T), jnp.int32),
        vm((D, T), F32),
        vm((D, T), BF16),
        vm((4, RY, T), BF16),
        vm((4, RY, 2 * T), BF16),
        vm((NBLK, 128, T), F32),
        vm((NBLK, 128, T), F32),
        vm((NVOC, 8, T), F32),
        vm((8, T), F32),
        vm((8, T), F32),
        vm((NVOC, 2 * T, 256), BF16),
        vm((NBLK, T, 128), BF16),
        vm((T, VP), BF16),
    ]
    scratch += [vm(chunk + (RY, 128), BF16)] * 6
    scratch += [vm(chunk + (RY, 128), F32), vm((NVOC, RY, 256), F32)]
    scratch += [vm((NVOC, 2 * R, 128), BF16)] * 6
    scratch += [vm((2, RV, T), BF16)] * 6
    scratch += [vm((2, RV, T), F32)] * 2
    scratch += [vm((RV, T), BF16)] * 2
    scratch += [pltpu.SMEM((NBLK,), jnp.int32)] * 2
    scratch += [dma((2,)), dma((4,)), dma((4,)), dma((4,)), dma((NVOC,)), dma((NVOC,)), dma(()), dma(())]
    scratch += [dma((NVOC,))] * 4
    scratch += [dma(chunk)] * 6 + [dma((NVOC,))] * 6 + [dma((2,))] * 6 + [dma(())] * 2
    anywhere = pl.BlockSpec(memory_space=pl.ANY)
    in_vmem = pl.BlockSpec(memory_space=pltpu.VMEM)
    d_hidden, blocks, inv = pl.pallas_call(
        kernel,
        out_shape=(
            jax.ShapeDtypeStruct((RV, T), BF16),
            jax.ShapeDtypeStruct((NBLK, R, 128), F32),
            jax.ShapeDtypeStruct((NBLK,), jnp.int32),
        ),
        in_specs=[pl.BlockSpec(memory_space=pltpu.SMEM), in_vmem, anywhere, anywhere, anywhere],
        out_specs=(in_vmem, in_vmem, pl.BlockSpec(memory_space=pltpu.SMEM)),
        scratch_shapes=scratch,
        compiler_params=pltpu.CompilerParams(
            collective_id=0, has_side_effects=True, vmem_limit_bytes=63 * 2**20
        ),
    )(slot_blocks, segment_ids, hidden, head.T, teacher_logp.T)
    d_hidden, d_head = pl.pallas_call(
        finish,
        out_shape=(jax.ShapeDtypeStruct((RV, T), BF16), jax.ShapeDtypeStruct((R, V), F32)),
        in_specs=[pl.BlockSpec(memory_space=pltpu.SMEM), in_vmem, in_vmem],
        out_specs=(in_vmem, in_vmem),
    )(inv, blocks, d_hidden)
    return d_hidden.T, d_head


def solution(mesh):
    placed = (P("tok", None), P(None, "voc"), P("tok", "voc"), P(), P("tok"))
    return jax.shard_map(
        body,
        mesh=mesh,
        in_specs=placed,
        out_specs=(P("tok", "voc"), P("tok", "voc")),
        check_vma=False,
    )
```

```python
import jax
import jax.numpy as jnp
from jax import lax
from jax.experimental import pallas as pl
from jax.experimental.pallas import tpu as pltpu
from jax.sharding import PartitionSpec as P

MESH = pl.DeviceIdType.MESH
F32 = jnp.float32
BF16 = jnp.bfloat16

NTOK = 32
NVOC = 8
T = 384
D = 2304
V = 2000
VP = 2048
NBLK = 16
BC = 125
LAST = V - 15 * 128
R = D // NTOK
RY = 4 * R
RV = D // NVOC
SEGS = 64
SEG_WEIGHT = 192.0
CAP = 30.0
SCALE = 1024.0

ORDER = (0, 1, 2, 7, 6, 3, 4, 5)
AHEAD = 8
LAG_C1 = 2
LAG_C2 = 3
LAG_C3 = 4
LAG_C4 = 5
TICKS = 8 + LAG_C4
TICK_H = 4


def dot(a, b):
    return jnp.dot(a, b, preferred_element_type=F32)


def dot_nt(a, b):
    return lax.dot_general(a, b, (((1,), (1,)), ((), ())), preferred_element_type=F32)


def kernel(
    slot, seg, hid_h, head_h, tea_h, dhid_o, fin, inv,
    tea_v, hid_v, head_v, tea32, nat32, tblk, tsend, trec, idb, h32, htn, hsend, ht,
    pblk, qblk, tots, arow, wrow, gc, gslot, gnat,
    yfar_s, yfar_r, ydir_s, ydir_r, yst_s, yst_r, ymid, yown,
    zfar_s, zfar_r, zdir_s, zdir_r, zst_s, zst_r,
    xfar_s, xfar_r, xdir_s, xdir_r, xst_s, xst_r, xmid, xown, zl_s, zl_r,
    snd, blk,
    lsem, hd_sem, id_ss, id_rs, t_ss, t_rs, ht_ss, ht_rs, tot_ss, tot_rs, g_ss, g_rs,
    yfar_ss, yfar_rs, ydir_ss, ydir_rs, yst_ss, yst_rs,
    zfar_ss, zfar_rs, zdir_ss, zdir_rs, zst_ss, zst_rs,
    xfar_ss, xfar_rs, xdir_ss, xdir_rs, xst_ss, xst_rs, zl_ss, zl_rs,
):
    t = lax.axis_index("tok")
    v = lax.axis_index("voc")
    c = lax.rem(t, 2)
    y = lax.rem(lax.div(t, 2), 4)
    zh = lax.div(t, 8)
    x = lax.div(v, 2)
    zl = lax.rem(v, 2)

    def at_y(step):
        return (zh * 8 + lax.rem(y + step + 4, 4) * 2 + c, v)

    def at_z(step):
        return (lax.rem(zh + step + 4, 4) * 8 + y * 2 + c, v)

    def at_x(step):
        return (t, lax.rem(x + step + 4, 4) * 2 + zl)

    sibling = (t + 1 - 2 * c, v)
    zl_peer = (t, v + 1 - 2 * zl)

    def at_v(step):
        return (t, lax.rem(v + step, NVOC))

    def at_t(step):
        return (lax.rem(t + step + NTOK, NTOK), v)

    def send(src, dst, ss, rs, device):
        return pltpu.make_async_remote_copy(
            src_ref=src, dst_ref=dst, send_sem=ss, recv_sem=rs, device_id=device, device_id_type=MESH
        )

    id_steps = (1, -1, 2, -2)

    barrier = pltpu.get_barrier_semaphore()
    partners = [sibling, at_y(1), at_y(-1), at_z(1), at_z(-1)]
    partners += [at_v(s) for s in range(1, NVOC)] + [at_t(s) for s in id_steps]
    for device in partners:
        pl.semaphore_signal(barrier, inc=1, device_id=device, device_id_type=MESH)

    tea_copy = pltpu.make_async_copy(tea_h, tea_v.at[pl.ds(0, V)], lsem.at[0])
    hid_copy = pltpu.make_async_copy(hid_h, hid_v, lsem.at[1])

    def head_copy(p):
        rows = pl.ds(p * 512, min(512, V - p * 512))
        return pltpu.make_async_copy(head_h.at[rows], head_v.at[rows], hd_sem.at[p])

    tea_copy.start()
    hid_copy.start()

    idb[0] = jnp.broadcast_to(seg[...].reshape(1, T), (8, T))

    tea_v[V:VP, :] = jnp.zeros((VP - V, T), BF16)
    head_v[V:VP, :] = jnp.zeros((VP - V, D), BF16)
    tea_copy.wait()
    head_copy(0).start()
    head_copy(1).start()

    def fold(values):
        return jnp.sum(values.reshape(values.shape[0] // 8, 8, T), axis=0)

    def tea_step(i, mass):
        rows = pl.ds(pl.multiple_of(i * 80, 80), 80)
        tile = tea_v[rows, :].astype(F32)
        tea32[rows, :] = tile
        return mass + fold(jnp.exp(tile))

    mass_part = lax.fori_loop(0, V // 80, tea_step, jnp.zeros((8, T), F32))
    tea32[V:VP, :] = jnp.zeros((VP - V, T), F32)

    def offset(k):
        out = jnp.int32(0)
        for i in range(1, NVOC):
            out = jnp.where(k == i, ORDER[i], out)
        return out

    @pl.loop(0, NVOC)
    def _(d):
        low = lax.rem(v + NVOC - offset(d), NVOC) * NBLK
        first = jnp.int32(0)
        last = jnp.int32(0)
        for j in range(NBLK):
            e = slot[v * NBLK + j]
            last = jnp.where((e >= low) & (e < low + NBLK), j, last)
            e = slot[v * NBLK + NBLK - 1 - j]
            first = jnp.where((e >= low) & (e < low + NBLK), NBLK - 1 - j, first)
        snd[2 * d] = first
        snd[2 * d + 1] = last

    @pl.loop(0, NVOC)
    def _(k):
        base = lax.rem(v + offset(k), NVOC) * NBLK
        low = v * NBLK
        first = jnp.int32(0)
        last = jnp.int32(0)
        for j in range(NBLK):
            e = slot[base + j]
            last = jnp.where((e >= low) & (e < low + NBLK), e - low, last)
            e = slot[base + NBLK - 1 - j]
            first = jnp.where((e >= low) & (e < low + NBLK), e - low, first)
        blk[2 * k] = first
        blk[2 * k + 1] = last

    @pl.loop(0, NBLK)
    def _(b):
        place = jnp.int32(0)
        for s in range(NBLK):
            place = jnp.where(blk[s] == b, s, place)
        inv[b] = place

    hid_copy.wait()

    @pl.loop(0, D // 128)
    def _(j):
        off = pl.multiple_of(j * 128, 128)
        turned = hid_v[:, pl.ds(off, 128)].astype(F32).T
        h32[pl.ds(off, 128), :] = turned
        htn[pl.ds(off, 128), :] = turned.astype(BF16)

    total_part = jnp.zeros((8, T), F32)
    valid = lax.broadcasted_iota(jnp.int32, (128, T), 0) < BC
    for p in range(5):
        if p < 4:
            head_copy(p).wait()
            if p < 2:
                head_copy(p + 2).start()
            nat32[p * 512 : p * 512 + 512, :] = dot(head_v[p * 512 : p * 512 + 512, :], htn[...])
        for b in range(4 * p - 4, 4 * p):
            if b < 0:
                continue
            th = jnp.tanh(nat32[b * BC : b * BC + 128, :] * (1.0 / CAP))
            shifted = jnp.exp(CAP * th - CAP)
            slope = 1.0 - th * th
            pblk[b] = shifted * slope
            qblk[b] = slope
            total_part += fold(jnp.where(valid, shifted, 0.0))

    sub = lax.broadcasted_iota(jnp.int32, (8, T), 0)
    total_row = jnp.sum(total_part, axis=0, keepdims=True)
    mass_row = jnp.sum(mass_part, axis=0, keepdims=True)
    tots[0] = jnp.where(sub == 0, total_row, mass_row)

    def tot_send(d):
        return send(tots.at[0], tots.at[NVOC - d], tot_ss.at[d], tot_rs.at[NVOC - d], at_v(d))

    pl.semaphore_wait(barrier, len(partners))
    for d in range(1, NVOC):
        tot_send(d).start()

    def tea_send(k):
        back = NVOC - (ORDER[k] if isinstance(k, int) else offset(k))
        return send(tsend.at[k], trec.at[k], t_ss.at[k], t_rs.at[k], at_v(back))

    def id_send(i):
        return send(idb.at[0], idb.at[i + 1], id_ss.at[i], id_rs.at[i], at_t(id_steps[i]))

    for i in range(4):
        id_send(i).start()

    def pack(core, yy):
        parts = []
        for z in range(4):
            parts.append(h32[pl.ds(pl.multiple_of((8 * z + 2 * yy + core) * R, 8), R), :])
        return jnp.concatenate(parts, axis=0).astype(BF16)

    @pl.loop(0, 4)
    def _(yy):
        hsend[yy] = pack(1 - c, yy)

    ht_send = send(hsend, ht.at[:, :, pl.ds(T, T)], ht_ss, ht_rs, sibling)
    ht_send.start()

    @pl.loop(0, 4)
    def _(yy):
        ht[yy, :, 0:T] = pack(c, yy)

    for b in range(NBLK):
        tblk[b] = tea32[b * BC : b * BC + 128, :].astype(BF16)

    for d in range(NVOC):
        for r in range(2):
            target = trec.at[0] if d == 0 else tsend.at[d]
            target[r * 128 : r * 128 + 128, :] = tblk[snd[2 * d + r]]

    for k in range(1, AHEAD):
        tea_send(k).start()

    for i in range(4):
        id_send(i).wait_recv()
    segments = lax.broadcasted_iota(jnp.int32, (SEGS, T), 0)
    own_hit = segments == idb[0, 0:1, :]
    hits = own_hit.astype(F32)
    for i in range(1, 5):
        hits += (segments == idb[i, 0:1, :]).astype(F32)
    counts = jnp.sum(hits, axis=1, keepdims=True)
    seg_size = jnp.sum(jnp.where(own_hit, counts, 0.0), axis=0, keepdims=True)
    weight = (SCALE * SEG_WEIGHT) / seg_size
    wrow[...] = jnp.broadcast_to(weight, (8, T))

    for d in range(1, NVOC):
        tot_send(NVOC - d).wait_recv()
    sums = tots[0]
    for d in range(1, NVOC):
        sums += tots[d]
    ratio = weight * (sums[1:2, :] / sums[0:1, :])
    arow[...] = jnp.broadcast_to(ratio, (8, T))

    for k in range(AHEAD, NVOC):
        tea_send(k).start()
    ht_send.wait_recv()

    def g_send(k):
        return send(
            gc.at[k, pl.ds(0, T), :], gc.at[k, pl.ds(T, T), :], g_ss.at[k], g_rs.at[k], sibling
        )

    def yfar(k, r):
        return send(yfar_s.at[k, r], yfar_r.at[k, r], yfar_ss.at[k, r], yfar_rs.at[k, r], at_y(1 - 2 * r))

    def ydir(k, r):
        return send(ydir_s.at[k, r], ydir_r.at[k, r], ydir_ss.at[k, r], ydir_rs.at[k, r], at_y(2 * r - 1))

    def yst(k, r):
        return send(yst_s.at[k, r], yst_r.at[k, r], yst_ss.at[k, r], yst_rs.at[k, r], at_y(1 - 2 * r))

    def zway(k):
        return 1 - 2 * lax.rem(k, 2)

    def zfar(k):
        return send(zfar_s.at[k], zfar_r.at[k], zfar_ss.at[k], zfar_rs.at[k], at_z(zway(k)))

    def zdir(k):
        return send(zdir_s.at[k], zdir_r.at[k], zdir_ss.at[k], zdir_rs.at[k], at_z(-zway(k)))

    def zst(k):
        return send(zst_s.at[k], zst_r.at[k], zst_ss.at[k], zst_rs.at[k], at_z(zway(k)))

    def grads(k):
        @pl.when(k > 0)
        def _():
            tea_send(k).wait_recv()

        for r in range(2):
            b = blk[2 * k + r]
            prob = jnp.exp(trec[k, r * 128 : r * 128 + 128, :].astype(F32))
            grad = arow[0:1, :] * pblk[b] - wrow[0:1, :] * (prob * qblk[b])
            grad = grad.T.astype(BF16)
            gc[k, 0:T, r * 128 : r * 128 + 128] = grad
            gslot[2 * k + r] = grad

        g_send(k).start()

    def mm(k):
        g_send(k).wait_recv()
        far = dot(ht[lax.rem(y + 2, 4)], gc[k])
        for r in range(2):
            yfar_s[k, r] = far[:, r * 128 : r * 128 + 128].astype(BF16)
            yfar(k, r).start()
        part = dot(ht[lax.rem(y + 1, 4)], gc[k])
        ydir_s[k, 1] = part[:, 128:].astype(BF16)
        ydir(k, 1).start()
        ymid[k, 0] = part[:, :128]
        part = dot(ht[lax.rem(y + 3, 4)], gc[k])
        ydir_s[k, 0] = part[:, :128].astype(BF16)
        ydir(k, 0).start()
        ymid[k, 1] = part[:, 128:]
        yown[k] = dot(ht[y], gc[k])

    def c1(k):
        for r in range(2):
            yfar(k, r).wait_recv()
            yst_s[k, r] = (ymid[k, r] + yfar_r[k, r].astype(F32)).astype(BF16)
            yst(k, r).start()

    def zrows(k, step):
        rows = pl.ds(pl.multiple_of(lax.rem(zh + step + 4, 4) * R, 8), R)
        return jnp.concatenate([yown[k, rows, 0:128], yown[k, rows, 128:256]], axis=0)

    def c2(k):
        for r in range(2):
            ydir(k, r).wait_recv()
            yst(k, r).wait_recv()
            lanes = slice(r * 128, r * 128 + 128)
            yown[k, :, lanes] += ydir_r[k, r].astype(F32) + yst_r[k, r].astype(F32)
        zfar_s[k] = zrows(k, 2).astype(BF16)
        zfar(k).start()
        zdir_s[k] = zrows(k, -zway(k)).astype(BF16)
        zdir(k).start()

    def c3(k):
        zfar(k).wait_recv()
        zst_s[k] = (zrows(k, zway(k)) + zfar_r[k].astype(F32)).astype(BF16)
        zst(k).start()

    def c4(k):
        zdir(k).wait_recv()
        zst(k).wait_recv()
        done = zrows(k, 0) + (zdir_r[k].astype(F32) + zst_r[k].astype(F32))
        fin[2 * k] = done[0:R]
        fin[2 * k + 1] = done[R : 2 * R]

    def xfar(h):
        return send(xfar_s.at[h], xfar_r.at[h], xfar_ss.at[h], xfar_rs.at[h], at_x(1 - 2 * h))

    def xdir(h):
        return send(xdir_s.at[h], xdir_r.at[h], xdir_ss.at[h], xdir_rs.at[h], at_x(2 * h - 1))

    def xst(h):
        return send(xst_s.at[h], xst_r.at[h], xst_ss.at[h], xst_rs.at[h], at_x(1 - 2 * h))

    zlx = send(zl_s, zl_r, zl_ss, zl_rs, zl_peer)

    def natural():
        @pl.loop(0, T // 64)
        def _(i):
            rows = pl.ds(pl.multiple_of(i * 64, 64), 64)
            lane = lax.broadcasted_iota(jnp.int32, (64, 128), 1)

            def rolled(b):
                s = inv[b]
                block = gslot[s, rows, :].astype(F32)
                return pltpu.roll(block, 128 - 3 * b, 1) if b else block

            here = rolled(0)
            for q in range(NBLK):
                after = rolled(q + 1) if q < 15 else jnp.zeros((64, 128), F32)
                gnat[rows, q * 128 : q * 128 + 128] = jnp.where(
                    lane < BC - 3 * q, here, after
                ).astype(BF16)
                here = after

    def part_h(step, h):
        rows = pl.ds(pl.multiple_of((lax.rem(x + step, 4) * 2 + h) * RV, 16), RV)
        return h32[rows, :]

    def hm(low, high):
        @pl.loop(low, high)
        def _(j):
            cols = pl.ds(pl.multiple_of(j * 256, 256), 256)
            h32[cols, :] = dot(gnat[...], head_v[:, cols]).T

    def ha():
        natural()
        hm(0, 3)

    def h0():
        hm(6, 9)
        for h in range(2):
            xfar_s[h] = part_h(2, h).astype(BF16)
            xfar(h).start()

    def hd():
        xdir_s[1] = part_h(1, 1).astype(BF16)
        xdir(1).start()
        xdir_s[0] = part_h(3, 0).astype(BF16)
        xdir(0).start()

    def h1():
        xmid[0] = part_h(1, 0)
        xmid[1] = part_h(3, 1)
        for h in range(2):
            xfar(h).wait_recv()
            xst_s[h] = (xmid[h] + xfar_r[h].astype(F32)).astype(BF16)
            xst(h).start()
        for h in range(2):
            xown[h] = part_h(0, h)

    def h2():
        for h in range(2):
            xdir(h).wait_recv()
            xst(h).wait_recv()
            xown[h] += xdir_r[h].astype(F32) + xst_r[h].astype(F32)
        zl_s[...] = xown[1 - zl].astype(BF16)
        zlx.start()

    def h3():
        zlx.wait_recv()
        full = xown[zl] + zl_r[...].astype(F32)
        dhid_o[...] = full.astype(BF16)

    @pl.loop(0, TICKS)
    def _(n):
        def stage(f, lag):
            @pl.when((n >= lag) & (n < lag + NVOC))
            def _():
                f(n - lag)

        stage(c1, LAG_C1)

        @pl.when(n == 0)
        def _():
            grads(0)

        stage(mm, 0)

        @pl.when(n < 2)
        def _():
            grads(n + 1)

        @pl.when((n >= 2) & (n < 5))
        def _():
            grads(2 * n - 1)

        @pl.when((n >= 2) & (n < 4))
        def _():
            grads(2 * n)

        stage(c2, LAG_C2)
        stage(c3, LAG_C3)
        stage(c4, LAG_C4)
        pl.when(n == TICK_H)(ha)
        pl.when(n == TICK_H + 1)(lambda: hm(3, 6))
        pl.when(n == TICK_H + 2)(h0)
        pl.when(n == TICK_H + 3)(hd)
        pl.when(n == TICK_H + 3)(h1)
        pl.when(n == TICK_H + 6)(h2)
        pl.when(n == TICK_H + 8)(h3)

    for i in range(4):
        id_send(i).wait_send()
    for d in range(1, NVOC):
        tea_send(d).wait_send()
        tot_send(d).wait_send()
    ht_send.wait_send()

    @pl.loop(0, NVOC)
    def _(k):
        g_send(k).wait_send()
        for r in range(2):
            yfar(k, r).wait_send()
            ydir(k, r).wait_send()
            yst(k, r).wait_send()
        zfar(k).wait_send()
        zdir(k).wait_send()
        zst(k).wait_send()

    for h in range(2):
        xfar(h).wait_send()
        xdir(h).wait_send()
        xst(h).wait_send()
    zlx.wait_send()


def finish(inv, fin, dhid, dhid_o, dhead_o):
    lane = lax.broadcasted_iota(jnp.int32, (R, 128), 1)

    def rolled_out(b):
        block = fin[inv[b]]
        return pltpu.roll(block, 128 - 3 * b, 1) if b else block

    here = rolled_out(0)
    for q in range(NBLK):
        after = rolled_out(q + 1) if q < 15 else here
        tile = jnp.where(lane < BC - 3 * q, here, after)
        if q < 15:
            dhead_o[:, q * 128 : q * 128 + 128] = tile
        else:
            dhead_o[:, 1920:V] = tile[:, 0:LAST]
        here = after
    dhid_o[...] = dhid[...]


def body(hidden, head, teacher_logp, slot_blocks, segment_ids):
    vm = pltpu.VMEM
    dma = pltpu.SemaphoreType.DMA
    chunk = (NVOC, 2)
    scratch = [
        vm((VP, T), BF16),
        vm((T, D), BF16),
        vm((VP, D), BF16),
        vm((VP, T), F32),
        vm((VP, T), F32),
        vm((NBLK, 128, T), BF16),
        vm((NVOC, 256, T), BF16),
        vm((NVOC, 256, T), BF16),
        vm((5, 8, T), jnp.int32),
        vm((D, T), F32),
        vm((D, T), BF16),
        vm((4, RY, T), BF16),
        vm((4, RY, 2 * T), BF16),
        vm((NBLK, 128, T), F32),
        vm((NBLK, 128, T), F32),
        vm((NVOC, 8, T), F32),
        vm((8, T), F32),
        vm((8, T), F32),
        vm((NVOC, 2 * T, 256), BF16),
        vm((NBLK, T, 128), BF16),
        vm((T, VP), BF16),
    ]
    scratch += [vm(chunk + (RY, 128), BF16)] * 6
    scratch += [vm(chunk + (RY, 128), F32), vm((NVOC, RY, 256), F32)]
    scratch += [vm((NVOC, 2 * R, 128), BF16)] * 6
    scratch += [vm((2, RV, T), BF16)] * 6
    scratch += [vm((2, RV, T), F32)] * 2
    scratch += [vm((RV, T), BF16)] * 2
    scratch += [pltpu.SMEM((NBLK,), jnp.int32)] * 2
    scratch += [dma((2,)), dma((4,)), dma((4,)), dma((4,)), dma((NVOC,)), dma((NVOC,)), dma(()), dma(())]
    scratch += [dma((NVOC,))] * 4
    scratch += [dma(chunk)] * 6 + [dma((NVOC,))] * 6 + [dma((2,))] * 6 + [dma(())] * 2
    anywhere = pl.BlockSpec(memory_space=pl.ANY)
    in_vmem = pl.BlockSpec(memory_space=pltpu.VMEM)
    d_hidden, blocks, inv = pl.pallas_call(
        kernel,
        out_shape=(
            jax.ShapeDtypeStruct((RV, T), BF16),
            jax.ShapeDtypeStruct((NBLK, R, 128), F32),
            jax.ShapeDtypeStruct((NBLK,), jnp.int32),
        ),
        in_specs=[pl.BlockSpec(memory_space=pltpu.SMEM), in_vmem, anywhere, anywhere, anywhere],
        out_specs=(in_vmem, in_vmem, pl.BlockSpec(memory_space=pltpu.SMEM)),
        scratch_shapes=scratch,
        compiler_params=pltpu.CompilerParams(
            collective_id=0, has_side_effects=True, vmem_limit_bytes=63 * 2**20
        ),
    )(slot_blocks, segment_ids, hidden, head.T, teacher_logp.T)
    d_hidden, d_head = pl.pallas_call(
        finish,
        out_shape=(jax.ShapeDtypeStruct((RV, T), BF16), jax.ShapeDtypeStruct((R, V), F32)),
        in_specs=[pl.BlockSpec(memory_space=pltpu.SMEM), in_vmem, in_vmem],
        out_specs=(in_vmem, in_vmem),
    )(inv, blocks, d_hidden)
    return d_hidden.T, d_head


def solution(mesh):
    placed = (P("tok", None), P(None, "voc"), P("tok", "voc"), P(), P("tok"))
    return jax.shard_map(
        body,
        mesh=mesh,
        in_specs=placed,
        out_specs=(P("tok", "voc"), P("tok", "voc")),
        check_vma=False,
    )
```
